256 devices in a mesh: store: 32 (over y, x, core), trainer: 8 (over z).
Axes of the slice: x: 4, y: 4, z: 8, core: 2. Of those that a mesh axis runs over, the one named last changes fastest.
Arguments:
- features: bfloat16 [131072, 768], P('store'), may hold values from -6 to 6
- self_one: bfloat16 [768, 512], replicated, may hold values from -0.21875 to 0.21875
- neigh_one: bfloat16 [768, 512], replicated, may hold values from -0.21875 to 0.21875
- self_two: bfloat16 [512, 153], replicated, may hold values from -0.25 to 0.25
- neigh_two: bfloat16 [512, 153], replicated, may hold values from -0.25 to 0.25
- bucket_counts: int32 [2, 256, 32], P(None, ('store', 'trainer')), may hold values from 4 to 16, as said below
- request_rows: int32 [2, 256, 32, 16], P(None, ('store', 'trainer')), may hold values from 0 to 4095, as said below
- layer_targets: int32 [2, 131072], P(None, ('store', 'trainer')), may hold values from 0 to 511, as said below
- inner_slots: int32 [2, 131072, 10], P(None, ('store', 'trainer')), may hold values from 0 to 511, as said below
- outer_slots: int32 [2, 16384, 15], P(None, ('store', 'trainer')), may hold values from 0 to 511
- outer_degree: int32 [2, 16384], P(None, ('store', 'trainer')), may hold values from 0 to 15
- cotangent: bfloat16 [2, 16384, 153], P(None, ('store', 'trainer')), may hold values from -0.046875 to 0.046875
Outputs:
- logits: float32 [2, 16384, 153], P(None, ('store', 'trainer'))
- grad_self_one: float32 [768, 512], replicated
- grad_neigh_one: float32 [768, 512], replicated
- grad_self_two: float32 [512, 153], replicated
- grad_neigh_two: float32 [512, 153], replicated
The draws below stay inside these ranges and needn't reach their ends.
Inputs may be any that keep to these rules, and one draw needn't show every extreme that they name: Slots 0 to bucket_counts[b, d, o] - 1 of owner o's bucket are live. In every minibatch one owner's bucket is full (16) from every device, and every other bucket has fewer than 16 live slots. `request_rows`: the 16 rows of one device's bucket for one owner are distinct; some rows of an owner are asked for by many devices. `layer_targets`: every entry is a live frontier slot of its minibatch and device. `inner_slots`: every entry is a frontier slot of its minibatch and device; entries whose slot is not live are padding and take no part in the mean.
All inputs are finite; a program needn't handle non-finite values.
Results may differ from the reference program's by a relative error of at most 0.0041.
Values may be sent and summed in bfloat16 or wider, within the bound.
No kernel may reach another device: no remote copies, remote signals or barrier semaphores. Data moves between devices by JAX's collectives and lax.ppermute only.
A program may use at most 192 MiB of HBM per device.

```python
import jax
import jax.numpy as jnp
from jax import lax

D = 768
HIDDEN_SIZE = 512
CLASSES = 153
FAN1 = 15
FAN2 = 10
BATCHES = 2
SEEDS = 64
CAP = 16
ROWS_DEV = 4096
TARGETS = 512
NODES = 131072
N_STORE = 32
N_TRAINER = 8
DEVICES = 256


def counts_table(key):
    workers = N_STORE * N_TRAINER
    key_hot, key_draw, key_full = jax.random.split(jax.random.fold_in(key, 11), 3)
    grid_shape = (BATCHES, workers, N_STORE)
    hotness = jax.random.randint(key_hot, grid_shape, 0, 4) == 0
    lowest = jnp.where(hotness, CAP // 2, CAP // 4)
    highest = jnp.where(hotness, CAP, CAP // 2 + 1)
    drawn_counts = jax.random.randint(key_draw, grid_shape, lowest, highest)
    full_owner = jax.random.randint(key_full, (BATCHES, 1, 1), 0, N_STORE)
    owners = jnp.arange(N_STORE, dtype=jnp.int32)[None, None, :]
    return jnp.where(owners == full_owner, CAP, drawn_counts).astype(jnp.int32)


def live_pick(key, counts, tail_shape):
    key_owner, key_slot = jax.random.split(key)
    workers = counts.shape[1]
    owner_index = jax.random.randint(key_owner, (BATCHES, workers) + tail_shape, 0, N_STORE)
    flat_owner = owner_index.reshape(BATCHES, workers, -1)
    slot_limit = jnp.take_along_axis(counts, flat_owner, axis=2).reshape(owner_index.shape)
    slot_index = jax.random.randint(key_slot, owner_index.shape, 0, slot_limit)
    return owner_index * CAP + slot_index


def draw_bucket_counts(key, part):
    return counts_table(key)


def draw_request_rows(key, part):
    key = jax.random.fold_in(key, 5)
    workers = N_STORE * N_TRAINER
    row_ids = jnp.arange(ROWS_DEV, dtype=jnp.int32)
    end_rows = (row_ids == 0) | (row_ids == ROWS_DEV - 1)

    def one_batch(batch_key):
        key_rank, key_score = jax.random.split(batch_key)
        owner_keys = jax.random.split(key_rank, N_STORE)
        ranks = jax.vmap(lambda owner_key: jax.random.permutation(owner_key, ROWS_DEV))(owner_keys).astype(jnp.int32)
        weight = (262144 // (ranks + 1) + 1).astype(jnp.int32)
        device_keys = jax.random.split(key_score, workers)

        def one_device(device_key):
            scores = jax.random.randint(device_key, (N_STORE, ROWS_DEV), 0, weight)
            scores = scores * ROWS_DEV + row_ids[None, :]
            scores = jnp.where(end_rows[None, :], 2140000000 + row_ids[None, :], scores)
            return lax.top_k(scores, CAP)[1].astype(jnp.int32)
        return lax.map(one_device, device_keys)
    return lax.map(one_batch, jax.random.split(key, BATCHES)).astype(jnp.int32)


def draw_layer_targets(key, part):
    counts = counts_table(key)
    key = jax.random.fold_in(key, 2)
    return live_pick(key, counts, (TARGETS,)).astype(jnp.int32).reshape(BATCHES, -1)


def draw_inner_slots(key, part):
    counts = counts_table(key)
    key = jax.random.fold_in(key, 3)
    key_live, key_degree = jax.random.split(key)
    live_rows = live_pick(key_live, counts, (TARGETS, FAN2))
    degree = jax.random.randint(key_degree, (BATCHES, counts.shape[1], TARGETS, 1), 0, FAN2 + 1)
    spare_slot = (jnp.argmin(counts, axis=2) * CAP + CAP - 1)[:, :, None, None]
    column = jnp.arange(FAN2, dtype=jnp.int32)
    return jnp.where(column < degree, live_rows, spare_slot).astype(jnp.int32).reshape(BATCHES, -1, FAN2)


def with_ends(entries, key, low, high):
    spot = [jax.random.randint(jax.random.fold_in(key, axis), (), 0, length) for axis, length in enumerate(entries.shape)]
    longest = entries.shape.index(max(entries.shape))
    beside = spot[:longest] + [(spot[longest] + 1) % entries.shape[longest]] + spot[longest + 1:]
    return entries.at[tuple(spot)].set(low).at[tuple(beside)].set(high)


def levels(stream_key, shape, shards, low, high):
    factor_of = 1.0
    for dim, shards_of in shards:
        heights = jax.random.uniform(jax.random.fold_in(jax.random.fold_in(stream_key, 6), dim), (shards_of,), jnp.float32, low / len(shards), high / len(shards))
        factor_of = factor_of * jnp.repeat(jnp.exp(heights), shape[dim] // shards_of).reshape((-1,) + (1,) * (len(shape) - 1 - dim))
    return factor_of


def noise(rng, dims, scale, limit, cuts=(), kind=jnp.bfloat16):
    entries = jax.random.normal(rng, dims, jnp.float32) * scale
    if len(cuts) > 0:
        entries = levels(rng, dims, cuts, -0.22, 0.18) * entries
    return jnp.clip(entries, min=-limit, max=limit).astype(kind)


def setup_inputs(seed: int = 0) -> dict:
    arg_keys = jax.random.split(jax.random.key(seed), 13)
    features = noise(arg_keys[0], (NODES, D), 1.0, 6.0, ((0, 32),))
    self_one = noise(arg_keys[1], (D, HIDDEN_SIZE), D ** -0.5, 0.21875)
    neigh_one = noise(arg_keys[2], (D, HIDDEN_SIZE), D ** -0.5, 0.21875)
    self_two = noise(arg_keys[3], (HIDDEN_SIZE, CLASSES), HIDDEN_SIZE ** -0.5, 0.25)
    neigh_two = noise(arg_keys[4], (HIDDEN_SIZE, CLASSES), HIDDEN_SIZE ** -0.5, 0.25)
    bucket_counts = draw_bucket_counts(jax.random.fold_in(arg_keys[12], 71), 0)
    request_rows = draw_request_rows(jax.random.fold_in(arg_keys[12], 71), 0)
    layer_targets = draw_layer_targets(jax.random.fold_in(arg_keys[12], 71), 0)
    inner_slots = draw_inner_slots(jax.random.fold_in(arg_keys[12], 71), 0)
    outer_slots = with_ends(jax.random.randint(arg_keys[9], (BATCHES, DEVICES * SEEDS, FAN1), 0, TARGETS), jax.random.fold_in(arg_keys[9], 1), 0, TARGETS - 1).astype(jnp.int32)
    outer_degree = with_ends(jax.random.randint(arg_keys[10], (BATCHES, DEVICES * SEEDS), 0, FAN1 + 1), jax.random.fold_in(arg_keys[10], 1), 0, FAN1).astype(jnp.int32)
    cotangent = noise(arg_keys[11], (BATCHES, DEVICES * SEEDS, CLASSES), (1.0 / (SEEDS * DEVICES) ** 0.5), 0.046875, ((1, 256),))
    return dict(features=features, self_one=self_one, neigh_one=neigh_one, self_two=self_two, neigh_two=neigh_two, bucket_counts=bucket_counts, request_rows=request_rows, layer_targets=layer_targets, inner_slots=inner_slots, outer_slots=outer_slots, outer_degree=outer_degree, cotangent=cotangent)


def contract_rows(left, right):
    return lax.dot_general(left, right, (((0,), (0,)), ((), ())), preferred_element_type=jnp.float32)


def contract_cols(left, right):
    return lax.dot_general(left, right, (((1,), (1,)), ((), ())), preferred_element_type=jnp.float32)


def silu_slope(values):
    sigmoid = jax.nn.sigmoid(values)
    return sigmoid * (1.0 + values * (1.0 - sigmoid))


def mean_rows(table, slots, weights):
    picked = table[slots].astype(jnp.float32)
    return jnp.sum(weights[:, :, None] * picked, axis=1)


def sage_pass(fetched, counts, layer_targets, inner_slots, outer_slots, outer_degree, cotangent, self_one, neigh_one, self_two, neigh_two):
    slot_count = fetched.shape[0]
    capacity = slot_count // counts.shape[0]
    live_slots = (jnp.arange(capacity, dtype=jnp.int32)[None, :] < counts[:, None]).reshape(slot_count).astype(jnp.float32)
    present = live_slots[inner_slots]
    inner_weight = present / jnp.maximum(jnp.sum(present, axis=1, keepdims=True), 1.0)
    inner_mean = mean_rows(fetched, inner_slots, inner_weight).astype(jnp.bfloat16)
    own_rows = fetched[layer_targets]
    pre_one = jnp.dot(own_rows, self_one, preferred_element_type=jnp.float32) + jnp.dot(inner_mean, neigh_one, preferred_element_type=jnp.float32)
    hidden_one = jax.nn.silu(pre_one).astype(jnp.bfloat16)
    seed_count = outer_slots.shape[0]
    fanout = outer_slots.shape[1]
    seed_rows = hidden_one[:seed_count]
    outer_present = (jnp.arange(fanout, dtype=jnp.int32)[None, :] < outer_degree[:, None]).astype(jnp.float32)
    outer_weight = outer_present / jnp.maximum(outer_degree[:, None].astype(jnp.float32), 1.0)
    outer_mean = mean_rows(hidden_one, outer_slots, outer_weight).astype(jnp.bfloat16)
    logits = jnp.dot(seed_rows, self_two, preferred_element_type=jnp.float32) + jnp.dot(outer_mean, neigh_two, preferred_element_type=jnp.float32)
    grad_self_two = contract_rows(seed_rows, cotangent)
    grad_neigh_two = contract_rows(outer_mean, cotangent)
    back_seed = contract_cols(cotangent, self_two)
    back_mean = contract_cols(cotangent, neigh_two)
    spread = (back_mean[:, None, :] * outer_weight[:, :, None]).reshape(seed_count * fanout, back_mean.shape[1])
    back_hidden = jnp.zeros((hidden_one.shape[0], back_mean.shape[1]), jnp.float32).at[outer_slots.reshape(-1)].add(spread)
    back_hidden = back_hidden.at[:seed_count].add(back_seed)
    back_pre = (back_hidden * silu_slope(pre_one)).astype(jnp.bfloat16)
    grad_self_one = contract_rows(own_rows, back_pre)
    grad_neigh_one = contract_rows(inner_mean, back_pre)
    return logits, (grad_self_one, grad_neigh_one, grad_self_two, grad_neigh_two)


def reference(features, self_one, neigh_one, self_two, neigh_two, bucket_counts, request_rows, layer_targets, inner_slots, outer_slots, outer_degree, cotangent):
    workers = N_STORE * N_TRAINER
    row_base = (jnp.arange(N_STORE, dtype=jnp.int32) * ROWS_DEV)[:, None]

    def one_device(summed, scanned):
        counts, requests, targets, inner, outer, degree, upstream = scanned
        fetched = features[(row_base + requests).reshape(-1)]
        logits, grads = sage_pass(fetched, counts, targets, inner, outer, degree, upstream, self_one, neigh_one, self_two, neigh_two)
        return jax.tree.map(jnp.add, summed, grads), logits

    summed = (jnp.zeros((D, HIDDEN_SIZE), jnp.float32), jnp.zeros((D, HIDDEN_SIZE), jnp.float32),
              jnp.zeros((HIDDEN_SIZE, CLASSES), jnp.float32), jnp.zeros((HIDDEN_SIZE, CLASSES), jnp.float32))
    logit_list = []
    for batch in range(BATCHES):
        scanned = (bucket_counts[batch], request_rows[batch],
                   layer_targets[batch].reshape(workers, TARGETS),
                   inner_slots[batch].reshape(workers, TARGETS, FAN2),
                   outer_slots[batch].reshape(workers, SEEDS, FAN1),
                   outer_degree[batch].reshape(workers, SEEDS),
                   cotangent[batch].reshape(workers, SEEDS, CLASSES))
        summed, logits = lax.scan(one_device, summed, scanned)
        logit_list.append(logits.reshape(workers * SEEDS, CLASSES))
    return jnp.stack(logit_list), summed[0], summed[1], summed[2], summed[3]
```

```python
import functools

import jax
import jax.numpy as jnp
from jax import lax
from jax.experimental import pallas as pl
from jax.experimental.pallas import tpu as pltpu
from jax.sharding import Mesh, PartitionSpec as P

BF = jnp.bfloat16
F32 = jnp.float32
VMEM = pl.BlockSpec(memory_space=pltpu.VMEM)
SMEM = pl.BlockSpec(memory_space=pltpu.SMEM)
PARAMS = pltpu.CompilerParams(vmem_limit_bytes=56 * 1024 * 1024)


def nn(left, right):
    return lax.dot_general(left, right, (((1,), (0,)), ((), ())), preferred_element_type=F32)


def nt(left, right):
    return lax.dot_general(left, right, (((1,), (1,)), ((), ())), preferred_element_type=F32)


def tn(left, right):
    return lax.dot_general(left, right, (((0,), (0,)), ((), ())), preferred_element_type=F32)


def struct(shape, dtype):
    return jax.ShapeDtypeStruct(shape, dtype)


def cost(flops, size):
    return pl.CostEstimate(flops=flops, bytes_accessed=size, transcendentals=0)


def plan_kernel(
    counts_ref, targets_ref, inner_ref, outer_ref, degree_ref, cot_ref,
    self_one_ref, neigh_one_ref, self_two_ref, neigh_two_ref,
    own_ref, sum_ref, scale_ref, outer_sel_ref, outer_scale_ref, back_ref, self_t_ref, neigh_t_ref,
):
    batches, owners = counts_ref.shape
    slots, nodes = own_ref.shape[1:]
    fan_in = inner_ref.shape[1]
    fan_out, seeds = outer_ref.shape[1:]
    capacity = slots // owners
    block = 128
    self_t_ref[...] = self_one_ref[...].T
    neigh_t_ref[...] = neigh_one_ref[...].T
    for b in range(batches):
        degree = jnp.zeros((1, nodes), F32)
        for start in range(0, slots, block):
            slot = lax.broadcasted_iota(jnp.int32, (block, nodes), 0) + start
            own = jnp.where(slot == targets_ref[b : b + 1, :], 1.0, 0.0)
            own_ref[b, start : start + block, :] = own.astype(BF)
            total = jnp.zeros((block, nodes), F32)
            for k in range(fan_in):
                total += jnp.where(slot == inner_ref[b, k : k + 1, :], 1.0, 0.0)
            slot_col = lax.broadcasted_iota(jnp.int32, (block, owners), 0) + start
            owner_row = lax.broadcasted_iota(jnp.int32, (block, owners), 1)
            held = jnp.where(
                slot_col // capacity == owner_row, counts_ref[b : b + 1, :].astype(F32), 0.0
            )
            held = jnp.sum(held, axis=1, keepdims=True)
            place = lax.broadcasted_iota(jnp.int32, (block, 1), 0) % capacity
            total = jnp.where(place.astype(F32) < held, total, 0.0)
            degree += jnp.sum(total, axis=0, keepdims=True)
            sum_ref[b, start : start + block, :] = total.astype(BF)
        scale_ref[b, :, :] = 1.0 / jnp.maximum(degree, 1.0)

        seed_degree = degree_ref[b : b + 1, :]
        node = lax.broadcasted_iota(jnp.int32, (nodes, seeds), 0)
        chosen = jnp.zeros((nodes, seeds), F32)
        for k in range(fan_out):
            here = (node == outer_ref[b, k : k + 1, :]) & (seed_degree > k)
            chosen += jnp.where(here, 1.0, 0.0)
        outer_sel = chosen.astype(BF)
        outer_sel_ref[b, :, :] = outer_sel
        outer_scale = 1.0 / jnp.maximum(seed_degree.astype(F32), 1.0)
        outer_scale_ref[b, :, :] = outer_scale
        back_seed = nt(self_two_ref[...], cot_ref[b])
        back_mean = nt(neigh_two_ref[...], cot_ref[b]) * outer_scale
        high = back_mean.astype(BF)
        low = (back_mean - high.astype(F32)).astype(BF)
        back_ref[b, :, :] = nt(high, outer_sel) + nt(low, outer_sel)
        back_ref[b, :, 0:seeds] = back_ref[b, :, 0:seeds] + back_seed


def plan(counts, targets, inner, outer, degree, cot, self_one, neigh_one, self_two, neigh_two):
    batches, owners = counts.shape
    nodes = targets.shape[1]
    seeds = outer.shape[2]
    width, hidden = self_one.shape
    slots = nodes
    return pl.pallas_call(
        plan_kernel,
        out_shape=(
            struct((batches, slots, nodes), BF),
            struct((batches, slots, nodes), BF),
            struct((batches, 1, nodes), F32),
            struct((batches, nodes, seeds), BF),
            struct((batches, 1, seeds), F32),
            struct((batches, hidden, nodes), F32),
            struct((hidden, width), BF),
            struct((hidden, width), BF),
        ),
        in_specs=[VMEM] * 10,
        out_specs=[VMEM] * 8,
        compiler_params=PARAMS,
        cost_estimate=cost(200_000_000, 10_000_000),
        name="plan",
    )(counts, targets, inner, outer, degree, cot, self_one, neigh_one, self_two, neigh_two)


def serve_kernel(asked_ref, rows_ref, out_ref, wide, hot, total):
    step = pl.program_id(0)
    count = out_ref.shape[0]
    depth = rows_ref.shape[0]

    @pl.when(step == 0)
    def _():
        for start in range(0, count, 128):
            line = jnp.broadcast_to(asked_ref[:, start : start + 128], (128, 128))
            wide[start : start + 128, :] = line.T

    for start in range(0, depth, 128):
        place = lax.broadcasted_iota(jnp.int32, (count, 128), 1) + (step * depth + start)
        hot[:, start : start + 128] = jnp.where(wide[...] == place, 1.0, 0.0).astype(BF)
    part = nn(hot[...], rows_ref[...])

    @pl.when(step == 0)
    def _():
        total[...] = part

    @pl.when(step > 0)
    def _():
        total[...] += part

    @pl.when(step == pl.num_programs(0) - 1)
    def _():
        out_ref[...] = total[...].astype(BF)


def serve(asked, features):
    count = asked.shape[1]
    rows, width = features.shape
    depth = 1024
    return pl.pallas_call(
        serve_kernel,
        out_shape=struct((count, width), BF),
        grid=(rows // depth,),
        in_specs=[
            pl.BlockSpec((1, count), lambda i: (0, 0)),
            pl.BlockSpec((depth, width), lambda i: (i, 0)),
        ],
        out_specs=pl.BlockSpec((count, width), lambda i: (0, 0)),
        scratch_shapes=[
            pltpu.VMEM((count, 128), jnp.int32),
            pltpu.VMEM((count, depth), BF),
            pltpu.VMEM((count, width), F32),
        ],
        compiler_params=PARAMS,
        cost_estimate=cost(2 * count * rows * width, 10_000_000),
        name="serve",
    )(asked, features)


def pass_kernel(
    core_ref, fetched_ref, own_sel_ref, sum_sel_ref, scale_ref, outer_sel_ref, outer_scale_ref,
    back_ref, cot_ref, self_t_ref, neigh_t_ref, self_two_ref, neigh_two_ref,
    logits_ref, keep_ref, send_ref, own_t, mean_t, first, second, back_t,
):
    batches = fetched_ref.shape[1]
    slots = own_sel_ref.shape[1]
    width = self_t_ref.shape[1]
    hidden = self_t_ref.shape[0]
    seeds, classes = logits_ref.shape[1:]
    second[...] = jnp.zeros_like(second)
    for b in range(batches):
        table = fetched_ref[:, b].reshape(slots, width).T
        own_t[...] = nn(table, own_sel_ref[b]).astype(BF)
        mean_t[...] = (nn(table, sum_sel_ref[b]) * scale_ref[b]).astype(BF)
        pre = nn(self_t_ref[...], own_t[...]) + nn(neigh_t_ref[...], mean_t[...])
        gate = 1.0 / (1.0 + jnp.exp(-pre))
        hidden_t = (pre * gate).astype(BF)
        back_t[...] = (back_ref[b] * (gate * (1.0 + pre * (1.0 - gate)))).astype(BF)
        outer_t = (nn(hidden_t, outer_sel_ref[b]) * outer_scale_ref[b]).astype(BF)
        seed_t = hidden_t[:, 0:seeds]
        logits_ref[b, :, :] = tn(seed_t, self_two_ref[...]) + tn(outer_t, neigh_two_ref[...])
        self_grad = nn(seed_t, cot_ref[b])
        neigh_grad = nn(outer_t, cot_ref[b])
        half = hidden // 2
        for h in range(2):
            second[h, :, 0:classes] += self_grad[h * half : (h + 1) * half, :]
            second[h, :, half : half + classes] += neigh_grad[h * half : (h + 1) * half, :]
        if b == 0:
            first[0] = nt(own_t[...], back_t[...])
            first[1] = nt(mean_t[...], back_t[...])
        else:
            first[0] += nt(own_t[...], back_t[...])
            first[1] += nt(mean_t[...], back_t[...])
    core = core_ref[0]
    keep_ref[0:width, :] = first[core]
    keep_ref[width:, :] = second[core]
    send_ref[0:width, :] = first[1 - core].astype(BF)
    send_ref[width:, :] = second[1 - core].astype(BF)


def both_passes(core, fetched, planned, cot, self_two, neigh_two, logit_shape):
    own_sel, sum_sel, scale, outer_sel, outer_scale, back, self_t, neigh_t = planned
    batches = fetched.shape[1]
    hidden, width = self_t.shape
    nodes = own_sel.shape[2]
    half_rows = width + hidden // 2
    return pl.pallas_call(
        pass_kernel,
        out_shape=(
            struct(logit_shape, F32),
            struct((half_rows, hidden), F32),
            struct((half_rows, hidden), BF),
        ),
        in_specs=[SMEM] + [VMEM] * 12,
        out_specs=[VMEM] * 3,
        scratch_shapes=[
            pltpu.VMEM((width, nodes), BF),
            pltpu.VMEM((width, nodes), BF),
            pltpu.VMEM((2, width, hidden), F32),
            pltpu.VMEM((2, hidden // 2, hidden), F32),
            pltpu.VMEM((hidden, nodes), BF),
        ],
        compiler_params=PARAMS,
        cost_estimate=cost(6_000_000_000, 20_000_000),
        name="both_passes",
    )(
        core, fetched, own_sel, sum_sel, scale, outer_sel, outer_scale, back, cot,
        self_t, neigh_t, self_two, neigh_two,
    )


def add_kernel(keep_ref, got_ref, out_ref):
    out_ref[...] = (keep_ref[...] + got_ref[...].astype(F32)).astype(BF)


def add_pair(keep, got):
    return pl.pallas_call(
        add_kernel,
        out_shape=struct(keep.shape, BF),
        in_specs=[VMEM] * 2,
        out_specs=VMEM,
        compiler_params=PARAMS,
        cost_estimate=cost(keep.size, keep.size * 8),
        name="add_pair",
    )(keep, got)


def sum_kernel(parts_ref, out_ref):
    total = parts_ref[0].astype(F32)
    for i in range(1, parts_ref.shape[0]):
        total += parts_ref[i].astype(F32)
    total = total.astype(BF)
    for i in range(out_ref.shape[0]):
        out_ref[i] = total


def sum_parts(parts, copies):
    return pl.pallas_call(
        sum_kernel,
        out_shape=struct((copies,) + parts.shape[1:], BF),
        in_specs=[VMEM],
        out_specs=VMEM,
        compiler_params=PARAMS,
        cost_estimate=cost(parts.size, parts.size * 4),
        name="sum_parts",
    )(parts)


def unpack_kernel(core_ref, mine_ref, other_ref, self_one_ref, neigh_one_ref, self_two_ref, neigh_two_ref):
    width = self_one_ref.shape[0]
    half = mine_ref.shape[0] - width
    classes = self_two_ref.shape[1]

    def place(ref, one_ref, h):
        one_ref[...] = ref[0:width, :].astype(F32)
        tail = ref[width:, :].astype(F32)
        self_two_ref[h * half : (h + 1) * half, :] = tail[:, 0:classes]
        neigh_two_ref[h * half : (h + 1) * half, :] = tail[:, half : half + classes]

    @pl.when(core_ref[0] == 0)
    def _():
        place(mine_ref, self_one_ref, 0)
        place(other_ref, neigh_one_ref, 1)

    @pl.when(core_ref[0] != 0)
    def _():
        place(mine_ref, neigh_one_ref, 1)
        place(other_ref, self_one_ref, 0)


def unpack(core, mine, other, one_shape, two_shape):
    return pl.pallas_call(
        unpack_kernel,
        out_shape=(
            struct(one_shape, F32),
            struct(one_shape, F32),
            struct(two_shape, F32),
            struct(two_shape, F32),
        ),
        in_specs=[SMEM, VMEM, VMEM],
        out_specs=[VMEM] * 4,
        compiler_params=PARAMS,
        cost_estimate=cost(mine.size, mine.size * 12),
        name="unpack",
    )(core, mine, other)


def exchange(value, axes):
    return lax.all_to_all(value, axes, split_axis=0, concat_axis=0, tiled=True)


def swap_cores(value):
    return lax.ppermute(value, "core", [(0, 1), (1, 0)])


def body(
    chips, trainers,
    features, self_one, neigh_one, self_two, neigh_two, bucket_counts, request_rows,
    layer_targets, inner_slots, outer_slots, outer_degree, cotangent,
):
    batches, _, owners, capacity = request_rows.shape
    width, hidden = self_one.shape
    core = lax.axis_index("core").reshape(1).astype(jnp.int32)
    wanted = request_rows[:, 0].transpose(1, 0, 2).reshape(owners, batches * capacity)
    asked = exchange(wanted, ("chip", "core"))
    planned = plan(
        bucket_counts[:, 0],
        layer_targets,
        inner_slots.transpose(0, 2, 1),
        outer_slots.transpose(0, 2, 1),
        outer_degree,
        cotangent,
        self_one,
        neigh_one,
        self_two,
        neigh_two,
    )
    rows = serve(asked.reshape(1, -1), features)
    fetched = exchange(rows.reshape(owners, batches, capacity, width), ("chip", "core"))
    logits, keep, send = both_passes(
        core, fetched, planned, cotangent, self_two, neigh_two, cotangent.shape
    )
    half = add_pair(keep, swap_cores(send))
    piece = half.shape[0] // chips
    parts = exchange(half.reshape(chips, piece, hidden), "chip")
    parts = exchange(sum_parts(parts, trainers), "trainer")
    mine = exchange(sum_parts(parts, chips), "chip").reshape(chips * piece, hidden)
    grads = unpack(core, mine, swap_cores(mine), self_one.shape, self_two.shape)
    return (logits,) + tuple(grads)


def solution(mesh):
    stores, trainers = mesh.shape["store"], mesh.shape["trainer"]
    split = Mesh(
        mesh.devices.reshape(stores // 2, 2, trainers), ("chip", "core", "trainer")
    )
    store = ("chip", "core")
    every = ("chip", "core", "trainer")
    in_specs = (
        P(store, None),
        P(),
        P(),
        P(),
        P(),
        P(None, every, None),
        P(None, every, None, None),
        P(None, every),
        P(None, every, None),
        P(None, every, None),
        P(None, every),
        P(None, every, None),
    )
    out_specs = (P(None, every, None), P(), P(), P(), P())
    return jax.shard_map(
        functools.partial(body, stores // 2, trainers),
        mesh=split,
        in_specs=in_specs,
        out_specs=out_specs,
        check_vma=False,
    )
```

```python
import jax
import jax.numpy as jnp
from jax import lax
from jax.experimental import pallas as pl
from jax.experimental.pallas import tpu as pltpu
from jax.sharding import Mesh, PartitionSpec as P

BF = jnp.bfloat16
F32 = jnp.float32
VMEM = pl.BlockSpec(memory_space=pltpu.VMEM)
SMEM = pl.BlockSpec(memory_space=pltpu.SMEM)
LANES = 128
SUBLANES = 8


def nn(left, right):
    return lax.dot_general(left, right, (((1,), (0,)), ((), ())), preferred_element_type=F32)


def nt(left, right):
    return lax.dot_general(left, right, (((1,), (1,)), ((), ())), preferred_element_type=F32)


def tn(left, right):
    return lax.dot_general(left, right, (((0,), (0,)), ((), ())), preferred_element_type=F32)


def struct(shape, dtype):
    return jax.ShapeDtypeStruct(shape, dtype)


def params(mebibytes):
    return pltpu.CompilerParams(vmem_limit_bytes=mebibytes * 1024 * 1024)


def cost(flops, size):
    return pl.CostEstimate(flops=flops, bytes_accessed=size, transcendentals=0)


def plan_kernel(
    counts_ref, targets_ref, inner_ref, outer_ref, degree_ref, cot_ref,
    self_one_ref, neigh_one_ref, self_two_ref, neigh_two_ref,
    own_ref, sum_ref, scale_ref, outer_sel_ref, outer_scale_ref, back_ref, self_t_ref, neigh_t_ref,
    cot_t_ref,
):
    batches, owners = counts_ref.shape
    slots, nodes = own_ref.shape[1:]
    fan_in = inner_ref.shape[1]
    fan_out, seeds = outer_ref.shape[1:]
    capacity = slots // owners
    block = 128
    self_t_ref[...] = self_one_ref[...].T
    neigh_t_ref[...] = neigh_one_ref[...].T
    for b in range(batches):
        degree = jnp.zeros((1, nodes), F32)
        for start in range(0, slots, block):
            slot = lax.broadcasted_iota(jnp.int32, (block, nodes), 0) + start
            own = jnp.where(slot == targets_ref[b : b + 1, :], 1.0, 0.0)
            own_ref[b, start : start + block, :] = own.astype(BF)
            total = jnp.zeros((block, nodes), F32)
            for k in range(fan_in):
                total += jnp.where(slot == inner_ref[b, k : k + 1, :], 1.0, 0.0)
            slot_col = lax.broadcasted_iota(jnp.int32, (block, owners), 0) + start
            owner_row = lax.broadcasted_iota(jnp.int32, (block, owners), 1)
            held = jnp.where(
                slot_col // capacity == owner_row, counts_ref[b : b + 1, :].astype(F32), 0.0
            )
            held = jnp.sum(held, axis=1, keepdims=True)
            place = lax.broadcasted_iota(jnp.int32, (block, 1), 0) % capacity
            total = jnp.where(place.astype(F32) < held, total, 0.0)
            degree += jnp.sum(total, axis=0, keepdims=True)
            sum_ref[b, start : start + block, :] = total.astype(BF)
        scale_ref[b, :, :] = 1.0 / jnp.maximum(degree, 1.0)

        seed_degree = degree_ref[b : b + 1, :]
        node = lax.broadcasted_iota(jnp.int32, (nodes, seeds), 0)
        chosen = jnp.zeros((nodes, seeds), F32)
        for k in range(fan_out):
            here = (node == outer_ref[b, k : k + 1, :]) & (seed_degree > k)
            chosen += jnp.where(here, 1.0, 0.0)
        outer_sel = chosen.astype(BF)
        outer_sel_ref[b, :, :] = outer_sel
        outer_scale = 1.0 / jnp.maximum(seed_degree.astype(F32), 1.0)
        outer_scale_ref[b, :, :] = outer_scale
        cot_t = cot_ref[b].T
        cot_t_ref[b, :, :] = cot_t
        back_seed = tn(self_two_ref[...], cot_t)
        back_mean = tn(neigh_two_ref[...], cot_t) * outer_scale
        high = back_mean.astype(BF)
        low = (back_mean - high.astype(F32)).astype(BF)
        back_ref[b, :, :] = nt(high, outer_sel) + nt(low, outer_sel)
        back_ref[b, :, 0:seeds] = back_ref[b, :, 0:seeds] + back_seed


def plan(counts, targets, inner, outer, degree, cot, self_one, neigh_one, self_two, neigh_two):
    batches, owners = counts.shape
    nodes = targets.shape[1]
    seeds, classes = cot.shape[1:]
    width, hidden = self_one.shape
    slots = nodes
    return pl.pallas_call(
        plan_kernel,
        out_shape=(
            struct((batches, slots, nodes), BF),
            struct((batches, slots, nodes), BF),
            struct((batches, 1, nodes), F32),
            struct((batches, nodes, seeds), BF),
            struct((batches, 1, seeds), F32),
            struct((batches, hidden, nodes), F32),
            struct((hidden, width), BF),
            struct((hidden, width), BF),
            struct((batches, classes, seeds), BF),
        ),
        in_specs=[VMEM] * 10,
        out_specs=[VMEM] * 9,
        compiler_params=params(24),
        cost_estimate=cost(200_000_000, 10_000_000),
        name="plan",
    )(counts, targets, inner, outer, degree, cot, self_one, neigh_one, self_two, neigh_two)


def widen_kernel(rows_ref, out_ref):
    rows, width = rows_ref.shape
    for j in range(width // LANES):
        piece = rows_ref[:, j * LANES : (j + 1) * LANES]
        out_ref[pl.ds(j, rows, stride=SUBLANES), :] = piece.astype(F32)


def widen(features):
    rows, width = features.shape
    block = rows // 8
    return pl.pallas_call(
        widen_kernel,
        out_shape=struct((rows * SUBLANES, LANES), F32),
        grid=(rows // block,),
        in_specs=[pl.BlockSpec((block, width), lambda i: (i, 0))],
        out_specs=pl.BlockSpec((block * SUBLANES, LANES), lambda i: (i, 0)),
        compiler_params=params(10),
        cost_estimate=cost(rows * width, rows * width * 6),
        name="widen",
    )(features)


def serve_kernel(asked_ref, rows_ref, out_ref, picked):
    askers, each = asked_ref.shape
    count, width = out_ref.shape

    def one_asker(p, carry):
        for q in range(each):
            source = pl.multiple_of(asked_ref[p, q] * SUBLANES, SUBLANES)
            target = pl.multiple_of((p * each + q) * SUBLANES, SUBLANES)
            picked[pl.ds(target, SUBLANES), :] = rows_ref[pl.ds(source, SUBLANES), :]
        return carry

    lax.fori_loop(0, askers, one_asker, 0)
    for j in range(width // LANES):
        piece = picked[pl.ds(j, count, stride=SUBLANES), :]
        out_ref[:, j * LANES : (j + 1) * LANES] = piece.astype(BF)


def serve(asked, wide, width):
    count = asked.size
    return pl.pallas_call(
        serve_kernel,
        out_shape=struct((count, width), BF),
        in_specs=[SMEM, VMEM],
        out_specs=VMEM,
        scratch_shapes=[pltpu.VMEM((count * SUBLANES, LANES), F32)],
        compiler_params=params(26),
        cost_estimate=cost(count * width, count * width * 10),
        name="serve",
    )(asked, wide)


def pass_kernel(
    core_ref, fetched_ref, own_sel_ref, sum_sel_ref, scale_ref, outer_sel_ref, outer_scale_ref,
    back_ref, self_t_ref, neigh_t_ref, cot_t_ref, self_two_ref, neigh_two_ref,
    logits_ref, keep_ref, send_ref, own_t, mean_t, back_t, first, second,
):
    batches = fetched_ref.shape[1]
    slots = own_sel_ref.shape[1]
    width = self_t_ref.shape[1]
    hidden = self_t_ref.shape[0]
    seeds, classes = logits_ref.shape[1:]
    nodes = own_sel_ref.shape[2]
    second[:, classes:, :] = jnp.zeros((2, second.shape[1] - classes, hidden), F32)
    for b in range(batches):
        here = slice(b * nodes, (b + 1) * nodes)
        table = fetched_ref[:, b].reshape(slots, width).T
        own_t[:, here] = nn(table, own_sel_ref[b]).astype(BF)
        mean_t[:, here] = (nn(table, sum_sel_ref[b]) * scale_ref[b]).astype(BF)
        pre = nn(self_t_ref[...], own_t[:, here]) + nn(neigh_t_ref[...], mean_t[:, here])
        gate = 1.0 / (1.0 + jnp.exp(-pre))
        hidden_t = (pre * gate).astype(BF)
        back_t[:, here] = (back_ref[b] * (gate * (1.0 + pre * (1.0 - gate)))).astype(BF)
        outer_t = (nn(hidden_t, outer_sel_ref[b]) * outer_scale_ref[b]).astype(BF)
        seed_t = hidden_t[:, 0:seeds]
        logits_ref[b, :, :] = (nn(self_two_ref[...], seed_t) + nn(neigh_two_ref[...], outer_t)).T
        self_grad = nt(cot_t_ref[b], seed_t)
        neigh_grad = nt(cot_t_ref[b], outer_t)
        if b == 0:
            second[0, 0:classes, :] = self_grad
            second[1, 0:classes, :] = neigh_grad
        else:
            second[0, 0:classes, :] += self_grad
            second[1, 0:classes, :] += neigh_grad
    first[0] = nt(own_t[...], back_t[...])
    first[1] = nt(mean_t[...], back_t[...])
    core = core_ref[0]
    keep_ref[0:width, :] = first[core]
    keep_ref[width:, :] = second[core]
    send_ref[0:width, :] = first[1 - core].astype(BF)
    send_ref[width:, :] = second[1 - core].astype(BF)


def both_passes(core, fetched, planned, self_two, neigh_two, logit_shape):
    batches = fetched.shape[1]
    width = fetched.shape[3]
    hidden = self_two.shape[1]
    nodes = planned[0].shape[2]
    tail = hidden // 2
    return pl.pallas_call(
        pass_kernel,
        out_shape=(
            struct(logit_shape, F32),
            struct((width + tail, hidden), F32),
            struct((width + tail, hidden), BF),
        ),
        in_specs=[SMEM] + [VMEM] * 12,
        out_specs=[VMEM] * 3,
        scratch_shapes=[
            pltpu.VMEM((width, batches * nodes), BF),
            pltpu.VMEM((width, batches * nodes), BF),
            pltpu.VMEM((hidden, batches * nodes), BF),
            pltpu.VMEM((2, width, hidden), F32),
            pltpu.VMEM((2, tail, hidden), F32),
        ],
        compiler_params=params(32),
        cost_estimate=cost(6_000_000_000, 20_000_000),
        name="both_passes",
    )(core, fetched, *planned, self_two, neigh_two)


def add_kernel(keep_ref, got_ref, out_ref):
    out_ref[...] = (keep_ref[...] + got_ref[...].astype(F32)).astype(BF)


def add_pair(keep, got):
    return pl.pallas_call(
        add_kernel,
        out_shape=struct(keep.shape, BF),
        in_specs=[VMEM] * 2,
        out_specs=VMEM,
        compiler_params=params(6),
        cost_estimate=cost(keep.size, keep.size * 8),
        name="add_pair",
    )(keep, got)


def sum_kernel(parts_ref, out_ref):
    total = parts_ref[0].astype(F32)
    for i in range(1, parts_ref.shape[0]):
        total += parts_ref[i].astype(F32)
    out_ref[...] = total.astype(BF)


def sum_parts(parts):
    return pl.pallas_call(
        sum_kernel,
        out_shape=struct(parts.shape[1:], BF),
        in_specs=[VMEM],
        out_specs=VMEM,
        compiler_params=params(3),
        cost_estimate=cost(parts.size, parts.size * 4),
        name="sum_parts",
    )(parts)


def total_kernel(own_ref, next_ref, across_ref, last_ref, out_ref):
    near = own_ref[...].astype(F32) + across_ref[...].astype(F32)
    far = next_ref[...].astype(F32) + last_ref[...].astype(F32)
    total = (near + far).astype(BF)
    for i in range(out_ref.shape[0]):
        out_ref[i] = total


def total_copies(own, got, copies):
    return pl.pallas_call(
        total_kernel,
        out_shape=struct((copies,) + own.shape, BF),
        in_specs=[VMEM] * 4,
        out_specs=VMEM,
        compiler_params=params(3),
        cost_estimate=cost(own.size * copies, own.size * copies * 2),
        name="total_copies",
    )(own, *got)


def unpack_kernel(
    core_ref, mine_ref, other_ref, mine_tail_ref, other_tail_ref,
    self_one_ref, neigh_one_ref, self_two_ref, neigh_two_ref,
):
    classes = self_two_ref.shape[0]

    def place(mine, other, mine_tail, other_tail):
        mine[...] = mine_ref[...].astype(F32)
        other[...] = other_ref[...].astype(F32)

        @pl.when(pl.program_id(0) == 0)
        def _():
            mine_tail[...] = mine_tail_ref[0:classes, :].astype(F32)
            other_tail[...] = other_tail_ref[0:classes, :].astype(F32)

    @pl.when(core_ref[0] == 0)
    def _():
        place(self_one_ref, neigh_one_ref, self_two_ref, neigh_two_ref)

    @pl.when(core_ref[0] != 0)
    def _():
        place(neigh_one_ref, self_one_ref, neigh_two_ref, self_two_ref)


def unpack(core, mine, other, one_shape, two_shape):
    width, hidden = one_shape
    tail = mine.shape[0] - width
    steps = 4
    head = pl.BlockSpec((width // steps, hidden), lambda i: (i, 0))
    last = pl.BlockSpec((tail, hidden), lambda i: (width // tail, 0))
    two = pl.BlockSpec(two_shape, lambda i: (0, 0))
    return pl.pallas_call(
        unpack_kernel,
        out_shape=(
            struct(one_shape, F32),
            struct(one_shape, F32),
            struct(two_shape, F32),
            struct(two_shape, F32),
        ),
        grid=(steps,),
        in_specs=[SMEM, head, head, last, last],
        out_specs=[head, head, two, two],
        compiler_params=params(8),
        cost_estimate=cost(mine.size, mine.size * 12),
        name="unpack",
    )(core, mine, other, mine, other)


def exchange(value, axes):
    return lax.all_to_all(value, axes, split_axis=0, concat_axis=0, tiled=True)


def swap_cores(value):
    return lax.ppermute(value, "core", [(0, 1), (1, 0)])


def body(
    features, self_one, neigh_one, self_two, neigh_two, bucket_counts, request_rows,
    layer_targets, inner_slots, outer_slots, outer_degree, cotangent,
):
    batches, _, owners, capacity = request_rows.shape
    width, hidden = self_one.shape
    core = lax.axis_index("core").reshape(1).astype(jnp.int32)
    wanted = request_rows[:, 0].transpose(1, 0, 2).reshape(owners, batches * capacity)
    asked = exchange(wanted, ("chip", "core"))
    wide = widen(features)
    planned = plan(
        bucket_counts[:, 0],
        layer_targets,
        inner_slots.transpose(0, 2, 1),
        outer_slots.transpose(0, 2, 1),
        outer_degree,
        cotangent,
        self_one,
        neigh_one,
        self_two.T,
        neigh_two.T,
    )
    rows = serve(asked, wide, width)
    fetched = exchange(rows.reshape(owners, batches, capacity, width), ("chip", "core"))
    logits, keep, send = both_passes(
        core, fetched, planned, self_two.T, neigh_two.T, cotangent.shape
    )
    half = add_pair(keep, swap_cores(send))
    plane = ("chip", "near")
    parties = lax.axis_size(plane)
    far = lax.axis_size("far")
    piece = half.shape[0] // parties
    own = sum_parts(exchange(half.reshape(parties, piece, hidden), plane))
    got = [
        lax.ppermute(own, "far", [(i, (i + shift) % far) for i in range(far)])
        for shift in range(1, far)
    ]
    mine = exchange(total_copies(own, got, parties), plane).reshape(half.shape)
    grads = unpack(core, mine, swap_cores(mine), self_one.shape, self_two.T.shape)
    return (logits, grads[0], grads[1], grads[2].T, grads[3].T)


def solution(mesh):
    stores, trainers = mesh.shape["store"], mesh.shape["trainer"]
    split = Mesh(
        mesh.devices.reshape(stores // 2, 2, trainers // 2, 2), ("chip", "core", "far", "near")
    )
    store = ("chip", "core")
    every = ("chip", "core", "far", "near")
    in_specs = (
        P(store, None),
        P(),
        P(),
        P(),
        P(),
        P(None, every, None),
        P(None, every, None, None),
        P(None, every),
        P(None, every, None),
        P(None, every, None),
        P(None, every),
        P(None, every, None),
    )
    out_specs = (P(None, every, None), P(), P(), P(), P())
    return jax.shard_map(
        body, mesh=split, in_specs=in_specs, out_specs=out_specs, check_vma=False
    )
```

```python
import jax
import jax.numpy as jnp
from jax import lax
from jax.experimental import pallas as pl
from jax.experimental.pallas import tpu as pltpu
from jax.sharding import Mesh, PartitionSpec as P

BF = jnp.bfloat16
F32 = jnp.float32
VMEM = pl.BlockSpec(memory_space=pltpu.VMEM)
SMEM = pl.BlockSpec(memory_space=pltpu.SMEM)
ANY = pl.BlockSpec(memory_space=pl.ANY)
LANES = 128
SUBLANES = 8


def nn(left, right):
    return lax.dot_general(left, right, (((1,), (0,)), ((), ())), preferred_element_type=F32)


def nt(left, right):
    return lax.dot_general(left, right, (((1,), (1,)), ((), ())), preferred_element_type=F32)


def tn(left, right):
    return lax.dot_general(left, right, (((0,), (0,)), ((), ())), preferred_element_type=F32)


def struct(shape, dtype):
    return jax.ShapeDtypeStruct(shape, dtype)


def in_hbm(value):
    return pltpu.with_memory_space_constraint(value, pltpu.HBM)


def params(mebibytes):
    return pltpu.CompilerParams(vmem_limit_bytes=mebibytes * 1024 * 1024)


def cost(flops, size):
    return pl.CostEstimate(flops=flops, bytes_accessed=size, transcendentals=0)


def plan_kernel(
    counts_ref, targets_ref, inner_ref, outer_ref, degree_ref, cot_ref,
    self_one_ref, neigh_one_ref, self_two_ref, neigh_two_ref,
    own_ref, sum_ref, scale_ref, outer_sel_ref, outer_scale_ref, back_ref, self_t_ref, neigh_t_ref,
    cot_t_ref,
):
    batches, owners = counts_ref.shape
    slots, nodes = own_ref.shape[1:]
    fan_in = inner_ref.shape[1]
    fan_out, seeds = outer_ref.shape[1:]
    capacity = slots // owners
    block = 128
    self_t_ref[...] = self_one_ref[...].T
    neigh_t_ref[...] = neigh_one_ref[...].T
    for b in range(batches):
        degree = jnp.zeros((1, nodes), F32)
        for start in range(0, slots, block):
            slot = lax.broadcasted_iota(jnp.int32, (block, nodes), 0) + start
            own = jnp.where(slot == targets_ref[b : b + 1, :], 1.0, 0.0)
            own_ref[b, start : start + block, :] = own.astype(BF)
            total = jnp.zeros((block, nodes), F32)
            for k in range(fan_in):
                total += jnp.where(slot == inner_ref[b, k : k + 1, :], 1.0, 0.0)
            slot_col = lax.broadcasted_iota(jnp.int32, (block, owners), 0) + start
            owner_row = lax.broadcasted_iota(jnp.int32, (block, owners), 1)
            held = jnp.where(
                slot_col // capacity == owner_row, counts_ref[b : b + 1, :].astype(F32), 0.0
            )
            held = jnp.sum(held, axis=1, keepdims=True)
            place = lax.broadcasted_iota(jnp.int32, (block, 1), 0) % capacity
            total = jnp.where(place.astype(F32) < held, total, 0.0)
            degree += jnp.sum(total, axis=0, keepdims=True)
            sum_ref[b, start : start + block, :] = total.astype(BF)
        scale_ref[b, :, :] = 1.0 / jnp.maximum(degree, 1.0)

        seed_degree = degree_ref[b : b + 1, :]
        node = lax.broadcasted_iota(jnp.int32, (nodes, seeds), 0)
        chosen = jnp.zeros((nodes, seeds), F32)
        for k in range(fan_out):
            here = (node == outer_ref[b, k : k + 1, :]) & (seed_degree > k)
            chosen += jnp.where(here, 1.0, 0.0)
        outer_sel = chosen.astype(BF)
        outer_sel_ref[b, :, :] = outer_sel
        outer_scale = 1.0 / jnp.maximum(seed_degree.astype(F32), 1.0)
        outer_scale_ref[b, :, :] = outer_scale
        cot_t = cot_ref[b].T
        cot_t_ref[b, :, :] = cot_t
        back_seed = tn(self_two_ref[...], cot_t)
        back_mean = tn(neigh_two_ref[...], cot_t) * outer_scale
        high = back_mean.astype(BF)
        low = (back_mean - high.astype(F32)).astype(BF)
        back_ref[b, :, :] = nt(high, outer_sel) + nt(low, outer_sel)
        back_ref[b, :, 0:seeds] = back_ref[b, :, 0:seeds] + back_seed


def plan(counts, targets, inner, outer, degree, cot, self_one, neigh_one, self_two, neigh_two):
    batches, owners = counts.shape
    nodes = targets.shape[1]
    seeds, classes = cot.shape[1:]
    width, hidden = self_one.shape
    slots = nodes
    return pl.pallas_call(
        plan_kernel,
        out_shape=(
            pltpu.HBM((batches, slots, nodes), BF),
            pltpu.HBM((batches, slots, nodes), BF),
            pltpu.HBM((batches, 1, nodes), F32),
            pltpu.HBM((batches, nodes, seeds), BF),
            pltpu.HBM((batches, 1, seeds), F32),
            pltpu.HBM((batches, hidden, nodes), F32),
            pltpu.HBM((hidden, width), BF),
            pltpu.HBM((hidden, width), BF),
            pltpu.HBM((batches, classes, seeds), BF),
        ),
        in_specs=[VMEM] * 10,
        out_specs=[VMEM] * 9,
        compiler_params=params(24),
        cost_estimate=cost(200_000_000, 10_000_000),
        name="plan",
    )(counts, targets, inner, outer, degree, cot, self_one, neigh_one, self_two, neigh_two)


def serve_kernel(asked_ref, rows_ref, out_ref, landed, wide, sems):
    askers, each = asked_ref.shape
    rows, width = rows_ref.shape
    chunks = sems.shape[0]
    block = rows // chunks
    pieces = width // LANES

    def load(c):
        here = pl.ds(c * block, block)
        return pltpu.make_async_copy(rows_ref.at[here, :], landed.at[here, :], sems.at[c])

    for c in range(chunks):
        load(c).start()
    for c in range(chunks):
        load(c).wait()
        for j in range(pieces):
            piece = landed[pl.ds(c * block, block), j * LANES : (j + 1) * LANES]
            wide[j, pl.ds(SUBLANES + c * block, block), :] = piece.astype(F32)

    line = lax.broadcasted_iota(jnp.int32, (SUBLANES, LANES), 0)

    def one_asker(p, carry):
        for first in range(0, each, 2 * SUBLANES):
            tiles = []
            for half in range(2):
                base = first + half * SUBLANES
                starts = [asked_ref[p, base + i] + (SUBLANES - i) for i in range(SUBLANES)]
                for j in range(pieces):
                    tile = wide[j, pl.ds(starts[0], SUBLANES), :]
                    for i in range(1, SUBLANES):
                        tile = jnp.where(line == i, wide[j, pl.ds(starts[i], SUBLANES), :], tile)
                    tiles.append(tile)
            target = pl.ds(pl.multiple_of(p * each + first, 2 * SUBLANES), 2 * SUBLANES)
            for j in range(pieces):
                pair = jnp.concatenate([tiles[j], tiles[pieces + j]], axis=0)
                out_ref[target, j * LANES : (j + 1) * LANES] = pair.astype(BF)
        return carry

    lax.fori_loop(0, askers, one_asker, 0)


def serve(asked, features):
    count = asked.size
    rows, width = features.shape
    chunks = 8
    return pl.pallas_call(
        serve_kernel,
        out_shape=struct((count, width), BF),
        in_specs=[SMEM, ANY],
        out_specs=VMEM,
        scratch_shapes=[
            pltpu.VMEM((rows, width), BF),
            pltpu.VMEM((width // LANES, rows + 2 * SUBLANES, LANES), F32),
            pltpu.SemaphoreType.DMA((chunks,)),
        ],
        compiler_params=params(28),
        cost_estimate=cost(count * width, rows * width * 6),
        name="serve",
    )(asked, in_hbm(features))


def pass_kernel(
    core_ref, fetched_ref, own_sel_hbm, sum_sel_hbm, scale_hbm, outer_sel_hbm, outer_scale_hbm,
    back_hbm, self_t_hbm, neigh_t_hbm, cot_t_hbm, self_two_ref, neigh_two_ref,
    logits_ref, send_ref, inputs_t, back_t, second,
    own_sel_ref, sum_sel_ref, scale_ref, outer_sel_ref, outer_scale_ref, back_ref,
    self_t_ref, neigh_t_ref, cot_t_ref, sems,
):
    batches = fetched_ref.shape[1]
    slots, nodes = own_sel_ref.shape[1:]
    hidden, width = self_t_ref.shape
    seeds, classes = logits_ref.shape[1:]
    loads = []

    def load(source, target):
        copy = pltpu.make_async_copy(source, target, sems.at[len(loads)])
        loads.append(copy)
        return copy

    early = [
        [load(source.at[b], target.at[b]) for b in range(batches)]
        for source, target in (
            (own_sel_hbm, own_sel_ref), (sum_sel_hbm, sum_sel_ref), (back_hbm, back_ref),
        )
    ]
    scale = load(scale_hbm, scale_ref)
    weights = [load(self_t_hbm, self_t_ref), load(neigh_t_hbm, neigh_t_ref)]
    outer = [
        load(outer_sel_hbm, outer_sel_ref), load(outer_scale_hbm, outer_scale_ref),
        load(cot_t_hbm, cot_t_ref),
    ]
    early[0][0].start()
    early[1][0].start()
    scale.start()
    for copy in weights:
        copy.start()
    second[:, classes:, :] = jnp.zeros((2, second.shape[1] - classes, hidden), F32)
    for b in range(batches):
        here = slice(b * nodes, (b + 1) * nodes)
        table = fetched_ref[:, b].reshape(slots, width).T
        early[0][b].wait()
        own_t = nn(table, own_sel_ref[b]).astype(BF)
        inputs_t[0, :, here] = own_t
        if b == 0:
            early[2][0].start()
            for copy in outer:
                copy.start()
            scale.wait()
        early[1][b].wait()
        mean_t = (nn(table, sum_sel_ref[b]) * scale_ref[b]).astype(BF)
        inputs_t[1, :, here] = mean_t
        if b == 0:
            for later in range(1, batches):
                for copies in early:
                    copies[later].start()
            for copy in weights:
                copy.wait()
        pre = nn(self_t_ref[...], own_t) + nn(neigh_t_ref[...], mean_t)
        gate = 1.0 / (1.0 + jnp.exp(-pre))
        hidden_t = (pre * gate).astype(BF)
        early[2][b].wait()
        back_t[:, here] = (back_ref[b] * (gate * (1.0 + pre * (1.0 - gate)))).astype(BF)
        if b == 0:
            for copy in outer:
                copy.wait()
        outer_t = (nn(hidden_t, outer_sel_ref[b]) * outer_scale_ref[b]).astype(BF)
        seed_t = hidden_t[:, 0:seeds]
        logits_ref[b, :, :] = (nn(self_two_ref[...], seed_t) + nn(neigh_two_ref[...], outer_t)).T
        self_grad = nt(cot_t_ref[b], seed_t)
        neigh_grad = nt(cot_t_ref[b], outer_t)
        if b == 0:
            second[0, 0:classes, :] = self_grad
            second[1, 0:classes, :] = neigh_grad
        else:
            second[0, 0:classes, :] += self_grad
            second[1, 0:classes, :] += neigh_grad
    sent = 1 - core_ref[0]
    send_ref[0:width, :] = nt(inputs_t[sent], back_t[...]).astype(BF)
    send_ref[width:, :] = second[sent].astype(BF)


def both_passes(core, fetched, planned, self_two, neigh_two, logit_shape):
    batches = fetched.shape[1]
    width = fetched.shape[3]
    hidden = self_two.shape[1]
    nodes = planned[0].shape[2]
    tail = hidden // 2
    return pl.pallas_call(
        pass_kernel,
        out_shape=(
            struct(logit_shape, F32),
            struct((width + tail, hidden), BF),
            struct((2, width, batches * nodes), BF),
            struct((hidden, batches * nodes), BF),
            struct((2, tail, hidden), F32),
        ),
        in_specs=[SMEM, VMEM] + [ANY] * len(planned) + [VMEM] * 2,
        out_specs=[VMEM] * 5,
        scratch_shapes=[pltpu.VMEM(value.shape, value.dtype) for value in planned]
        + [pltpu.SemaphoreType.DMA((len(planned) + 3 * (batches - 1),))],
        compiler_params=params(40),
        cost_estimate=cost(4_500_000_000, 20_000_000),
        name="both_passes",
    )(core, fetched, *[in_hbm(value) for value in planned], self_two, neigh_two)


def keep_kernel(core_ref, inputs_t, back_t, second, keep_ref):
    core = core_ref[0]
    width = inputs_t.shape[1]
    keep_ref[0:width, :] = nt(inputs_t[core], back_t[...])
    keep_ref[width:, :] = second[core]


def keep_half(core, inputs_t, back_t, second):
    width, nodes = inputs_t.shape[1:]
    tail, hidden = second.shape[1:]
    return pl.pallas_call(
        keep_kernel,
        out_shape=struct((width + tail, hidden), F32),
        in_specs=[SMEM] + [VMEM] * 3,
        out_specs=VMEM,
        compiler_params=params(16),
        cost_estimate=cost(2 * width * hidden * nodes, 5_000_000),
        name="keep_half",
    )(core, inputs_t, back_t, second)


def add_kernel(keep_ref, got_ref, out_ref):
    out_ref[...] = (keep_ref[...] + got_ref[...].astype(F32)).astype(BF)


def add_pair(keep, got):
    return pl.pallas_call(
        add_kernel,
        out_shape=struct(keep.shape, BF),
        in_specs=[VMEM] * 2,
        out_specs=VMEM,
        compiler_params=params(6),
        cost_estimate=cost(keep.size, keep.size * 8),
        name="add_pair",
    )(keep, got)


def sum_kernel(parts_ref, out_ref):
    total = parts_ref[0].astype(F32)
    for i in range(1, parts_ref.shape[0]):
        total += parts_ref[i].astype(F32)
    out_ref[...] = total.astype(BF)


def sum_parts(parts):
    return pl.pallas_call(
        sum_kernel,
        out_shape=struct(parts.shape[1:], BF),
        in_specs=[VMEM],
        out_specs=VMEM,
        compiler_params=params(3),
        cost_estimate=cost(parts.size, parts.size * 4),
        name="sum_parts",
    )(parts)


def total_kernel(own_ref, next_ref, across_ref, last_ref, out_ref):
    near = own_ref[...].astype(F32) + across_ref[...].astype(F32)
    far = next_ref[...].astype(F32) + last_ref[...].astype(F32)
    total = (near + far).astype(BF)
    for i in range(out_ref.shape[0]):
        out_ref[i] = total


def total_copies(own, got, copies):
    return pl.pallas_call(
        total_kernel,
        out_shape=struct((copies,) + own.shape, BF),
        in_specs=[VMEM] * 4,
        out_specs=VMEM,
        compiler_params=params(3),
        cost_estimate=cost(own.size * copies, own.size * copies * 2),
        name="total_copies",
    )(own, *got)


def unpack_kernel(slot_ref, half_ref, *refs):
    self_one, neigh_one, self_two, neigh_two, head, tail, sems = refs[-7:]
    width = head.shape[0]
    classes = tail.shape[0]
    parts = sems.shape[0] - 1
    block = width // parts

    def place(one, two):
        copies = []
        for i in range(parts):
            here = slice(i * block, (i + 1) * block)
            head[here, :] = half_ref[here, :].astype(F32)
            copies.append(pltpu.make_async_copy(head.at[here], one.at[here], sems.at[i]))
            copies[-1].start()
        tail[...] = half_ref[width : width + classes, :].astype(F32)
        copies.append(pltpu.make_async_copy(tail, two, sems.at[parts]))
        copies[-1].start()
        for copy in copies:
            copy.wait()

    @pl.when(slot_ref[0] == 0)
    def _():
        place(self_one, self_two)

    @pl.when(slot_ref[0] != 0)
    def _():
        place(neigh_one, neigh_two)


def unpack(slot, half, one_shape, two_shape, placed=()):
    return pl.pallas_call(
        unpack_kernel,
        out_shape=tuple(pltpu.HBM(shape, F32) for shape in (one_shape,) * 2 + (two_shape,) * 2),
        in_specs=[SMEM, VMEM] + [ANY] * len(placed),
        out_specs=[ANY] * 4,
        scratch_shapes=[
            pltpu.VMEM(one_shape, F32),
            pltpu.VMEM(two_shape, F32),
            pltpu.SemaphoreType.DMA((5,)),
        ],
        input_output_aliases={2 + i: i for i in range(len(placed))},
        compiler_params=params(5),
        cost_estimate=cost(half.size, half.size * 6),
        name="unpack",
    )(slot, half, *[in_hbm(value) for value in placed])


def exchange(value, axes):
    return lax.all_to_all(value, axes, split_axis=0, concat_axis=0, tiled=True)


def swap_cores(value):
    return lax.ppermute(value, "core", [(0, 1), (1, 0)])


def body(
    features, self_one, neigh_one, self_two, neigh_two, bucket_counts, request_rows,
    layer_targets, inner_slots, outer_slots, outer_degree, cotangent,
):
    batches, _, owners, capacity = request_rows.shape
    width, hidden = self_one.shape
    core = lax.axis_index("core").reshape(1).astype(jnp.int32)
    wanted = request_rows[:, 0].transpose(1, 0, 2).reshape(owners, batches * capacity)
    asked = exchange(wanted, ("chip", "core"))
    planned = plan(
        bucket_counts[:, 0],
        layer_targets,
        inner_slots.transpose(0, 2, 1),
        outer_slots.transpose(0, 2, 1),
        outer_degree,
        cotangent,
        self_one,
        neigh_one,
        self_two.T,
        neigh_two.T,
    )
    rows = serve(asked, features)
    fetched = exchange(rows.reshape(owners, batches, capacity, width), ("chip", "core"))
    logits, send, inputs_t, back_t, second = both_passes(
        core, fetched, planned, self_two.T, neigh_two.T, cotangent.shape
    )
    got = swap_cores(send)
    half = add_pair(keep_half(core, inputs_t, back_t, second), got)
    plane = ("chip", "near")
    parties = lax.axis_size(plane)
    far = lax.axis_size("far")
    piece = half.shape[0] // parties
    own = sum_parts(exchange(half.reshape(parties, piece, hidden), plane))
    got = [
        lax.ppermute(own, "far", [(i, (i + shift) % far) for i in range(far)])
        for shift in range(1, far)
    ]
    mine = exchange(total_copies(own, got, parties), plane).reshape(half.shape)
    other = swap_cores(mine)
    shapes = (self_one.shape, self_two.T.shape)
    grads = unpack(1 - core, other, *shapes, unpack(core, mine, *shapes))
    return (logits, grads[0], grads[1], grads[2].T, grads[3].T)


def solution(mesh):
    stores, trainers = mesh.shape["store"], mesh.shape["trainer"]
    split = Mesh(
        mesh.devices.reshape(stores // 2, 2, trainers // 2, 2), ("chip", "core", "far", "near")
    )
    store = ("chip", "core")
    every = ("chip", "core", "far", "near")
    in_specs = (
        P(store, None),
        P(),
        P(),
        P(),
        P(),
        P(None, every, None),
        P(None, every, None, None),
        P(None, every),
        P(None, every, None),
        P(None, every, None),
        P(None, every),
        P(None, every, None),
    )
    out_specs = (P(None, every, None), P(), P(), P(), P())
    return jax.shard_map(
        body, mesh=split, in_specs=in_specs, out_specs=out_specs, check_vma=False
    )
```

```python
import jax
import jax.numpy as jnp
from jax import lax
from jax.experimental import pallas as pl
from jax.experimental.pallas import tpu as pltpu
from jax.sharding import Mesh, PartitionSpec as P

BF = jnp.bfloat16
F32 = jnp.float32
VMEM = pl.BlockSpec(memory_space=pltpu.VMEM)
SMEM = pl.BlockSpec(memory_space=pltpu.SMEM)
ANY = pl.BlockSpec(memory_space=pl.ANY)
LANES = 128
SUBLANES = 8


def nn(left, right):
    return lax.dot_general(left, right, (((1,), (0,)), ((), ())), preferred_element_type=F32)


def nt(left, right):
    return lax.dot_general(left, right, (((1,), (1,)), ((), ())), preferred_element_type=F32)


def tn(left, right):
    return lax.dot_general(left, right, (((0,), (0,)), ((), ())), preferred_element_type=F32)


def struct(shape, dtype):
    return jax.ShapeDtypeStruct(shape, dtype)


def in_hbm(value):
    return pltpu.with_memory_space_constraint(value, pltpu.HBM)


def params(mebibytes):
    return pltpu.CompilerParams(vmem_limit_bytes=mebibytes * 1024 * 1024)


def cost(flops, size):
    return pl.CostEstimate(flops=flops, bytes_accessed=size, transcendentals=0)


def plan_kernel(
    counts_ref, targets_ref, inner_ref, outer_ref, degree_ref, cot_ref,
    self_one_ref, neigh_one_ref, self_two_ref, neigh_two_ref,
    own_ref, sum_ref, scale_ref, outer_sel_ref, outer_scale_ref, back_ref, self_t_ref, neigh_t_ref,
    cot_t_ref,
):
    batches, owners = counts_ref.shape
    slots, nodes = own_ref.shape[1:]
    fan_in = inner_ref.shape[1]
    fan_out, seeds = outer_ref.shape[1:]
    capacity = slots // owners
    block = 128
    self_t_ref[...] = self_one_ref[...].T
    neigh_t_ref[...] = neigh_one_ref[...].T
    for b in range(batches):
        degree = jnp.zeros((1, nodes), F32)
        for start in range(0, slots, block):
            slot = lax.broadcasted_iota(jnp.int32, (block, nodes), 0) + start
            own = jnp.where(slot == targets_ref[b : b + 1, :], 1.0, 0.0)
            own_ref[b, start : start + block, :] = own.astype(BF)
            total = jnp.zeros((block, nodes), F32)
            for k in range(fan_in):
                total += jnp.where(slot == inner_ref[b, k : k + 1, :], 1.0, 0.0)
            slot_col = lax.broadcasted_iota(jnp.int32, (block, owners), 0) + start
            owner_row = lax.broadcasted_iota(jnp.int32, (block, owners), 1)
            held = jnp.where(
                slot_col // capacity == owner_row, counts_ref[b : b + 1, :].astype(F32), 0.0
            )
            held = jnp.sum(held, axis=1, keepdims=True)
            place = lax.broadcasted_iota(jnp.int32, (block, 1), 0) % capacity
            total = jnp.where(place.astype(F32) < held, total, 0.0)
            degree += jnp.sum(total, axis=0, keepdims=True)
            sum_ref[b, start : start + block, :] = total.astype(BF)
        scale_ref[b, :, :] = 1.0 / jnp.maximum(degree, 1.0)

        seed_degree = degree_ref[b : b + 1, :]
        node = lax.broadcasted_iota(jnp.int32, (nodes, seeds), 0)
        chosen = jnp.zeros((nodes, seeds), F32)
        for k in range(fan_out):
            here = (node == outer_ref[b, k : k + 1, :]) & (seed_degree > k)
            chosen += jnp.where(here, 1.0, 0.0)
        outer_sel = chosen.astype(BF)
        outer_sel_ref[b, :, :] = outer_sel
        outer_scale = 1.0 / jnp.maximum(seed_degree.astype(F32), 1.0)
        outer_scale_ref[b, :, :] = outer_scale
        cot_t = cot_ref[b].T
        cot_t_ref[b, :, :] = cot_t
        back_seed = tn(self_two_ref[...], cot_t)
        back_mean = tn(neigh_two_ref[...], cot_t) * outer_scale
        high = back_mean.astype(BF)
        low = (back_mean - high.astype(F32)).astype(BF)
        back_ref[b, :, :] = nt(high, outer_sel) + nt(low, outer_sel)
        back_ref[b, :, 0:seeds] = back_ref[b, :, 0:seeds] + back_seed


def plan(counts, targets, inner, outer, degree, cot, self_one, neigh_one, self_two, neigh_two):
    batches, owners = counts.shape
    nodes = targets.shape[1]
    seeds, classes = cot.shape[1:]
    width, hidden = self_one.shape
    slots = nodes
    return pl.pallas_call(
        plan_kernel,
        out_shape=(
            pltpu.HBM((batches, slots, nodes), BF),
            pltpu.HBM((batches, slots, nodes), BF),
            pltpu.HBM((batches, 1, nodes), F32),
            pltpu.HBM((batches, nodes, seeds), BF),
            pltpu.HBM((batches, 1, seeds), F32),
            pltpu.HBM((batches, hidden, nodes), F32),
            pltpu.HBM((hidden, width), BF),
            pltpu.HBM((hidden, width), BF),
            pltpu.HBM((batches, classes, seeds), BF),
        ),
        in_specs=[VMEM] * 10,
        out_specs=[VMEM] * 9,
        compiler_params=params(24),
        cost_estimate=cost(200_000_000, 10_000_000),
        name="plan",
    )(counts, targets, inner, outer, degree, cot, self_one, neigh_one, self_two, neigh_two)


def serve_kernel(asked_ref, rows_ref, out_ref, landed, wide, found, sems, out_sems):
    askers, each = asked_ref.shape
    rows, width = rows_ref.shape
    chunks = sems.shape[0]
    block = rows // chunks
    pieces = width // LANES

    def load(c):
        here = pl.ds(c * block, block)
        return pltpu.make_async_copy(rows_ref.at[here, :], landed.at[here, :], sems.at[c])

    for c in range(chunks):
        load(c).start()
    for c in range(chunks):
        load(c).wait()
        for j in range(pieces):
            piece = landed[pl.ds(c * block, block), j * LANES : (j + 1) * LANES]
            wide[j, pl.ds(SUBLANES + c * block, block), :] = piece.astype(F32)

    line = lax.broadcasted_iota(jnp.int32, (SUBLANES, LANES), 0)

    def one_asker(p, carry):
        for first in range(0, each, 2 * SUBLANES):
            tiles = []
            for half in range(2):
                base = first + half * SUBLANES
                starts = [asked_ref[p, base + i] + (SUBLANES - i) for i in range(SUBLANES)]
                for j in range(pieces):
                    tile = wide[j, pl.ds(starts[0], SUBLANES), :]
                    for i in range(1, SUBLANES):
                        tile = jnp.where(line == i, wide[j, pl.ds(starts[i], SUBLANES), :], tile)
                    tiles.append(tile)
            target = pl.ds(pl.multiple_of(p * each + first, 2 * SUBLANES), 2 * SUBLANES)
            for j in range(pieces):
                pair = jnp.concatenate([tiles[j], tiles[pieces + j]], axis=0)
                found[target, j * LANES : (j + 1) * LANES] = pair.astype(BF)
        return carry

    parts = out_sems.shape[0]
    count = askers // parts
    stores = []
    for part in range(parts):
        lax.fori_loop(part * count, (part + 1) * count, one_asker, 0)
        here = pl.ds(part * count * each, count * each)
        stores.append(pltpu.make_async_copy(found.at[here, :], out_ref.at[here, :], out_sems.at[part]))
        stores[-1].start()
    for store in stores:
        store.wait()


def serve(asked, features):
    count = asked.size
    rows, width = features.shape
    chunks = 8
    return pl.pallas_call(
        serve_kernel,
        out_shape=pltpu.HBM((count, width), BF),
        in_specs=[SMEM, ANY],
        out_specs=ANY,
        scratch_shapes=[
            pltpu.VMEM((rows, width), BF),
            pltpu.VMEM((width // LANES, rows + 2 * SUBLANES, LANES), F32),
            pltpu.VMEM((count, width), BF),
            pltpu.SemaphoreType.DMA((chunks,)),
            pltpu.SemaphoreType.DMA((4,)),
        ],
        compiler_params=params(28),
        cost_estimate=cost(count * width, rows * width * 6),
        name="serve",
    )(asked, in_hbm(features))


def pass_kernel(
    core_ref, fetched_ref, own_sel_hbm, sum_sel_hbm, scale_hbm, outer_sel_hbm, outer_scale_hbm,
    back_hbm, self_t_hbm, neigh_t_hbm, cot_t_hbm, self_two_ref, neigh_two_ref,
    logits_ref, send_ref, inputs_t, back_t, second,
    own_sel_ref, sum_sel_ref, scale_ref, outer_sel_ref, outer_scale_ref, back_ref,
    self_t_ref, neigh_t_ref, cot_t_ref, table_t, sems,
):
    batches = fetched_ref.shape[1]
    slots, nodes = own_sel_ref.shape[1:]
    hidden, width = self_t_ref.shape
    seeds, classes = logits_ref.shape[1:]
    pairs = (
        (own_sel_hbm, own_sel_ref), (sum_sel_hbm, sum_sel_ref), (back_hbm, back_ref),
        (scale_hbm, scale_ref), (self_t_hbm, self_t_ref), (neigh_t_hbm, neigh_t_ref),
        (outer_sel_hbm, outer_sel_ref), (outer_scale_hbm, outer_scale_ref),
        (cot_t_hbm, cot_t_ref),
    )
    split = [
        (source.at[b], target.at[b]) for b in range(batches) for source, target in pairs[:3]
    ]
    loads = [
        pltpu.make_async_copy(source, target, sems.at[i])
        for i, (source, target) in enumerate(split + list(pairs[3:]))
    ]
    count = len(split)
    first = loads[0:2] + loads[count : count + 3]
    rest = loads[2:count] + loads[count + 3 :]
    for copy in first + rest:
        copy.start()
    second[:, classes:, :] = jnp.zeros((2, second.shape[1] - classes, hidden), F32)
    for b in range(batches):
        table_t[b] = fetched_ref[:, b].reshape(slots, width).T

    def inputs(b):
        if b == 0:
            first[0].wait()
        own_t = nn(table_t[b], own_sel_ref[b]).astype(BF)
        if b == 0:
            first[1].wait()
            first[2].wait()
        mean_t = (nn(table_t[b], sum_sel_ref[b]) * scale_ref[b]).astype(BF)
        inputs_t[0, :, b * nodes : (b + 1) * nodes] = own_t
        inputs_t[1, :, b * nodes : (b + 1) * nodes] = mean_t
        if b == 0:
            first[3].wait()
            first[4].wait()
        return nn(self_t_ref[...], own_t) + nn(neigh_t_ref[...], mean_t)

    pre = inputs(0)
    for copy in rest:
        copy.wait()
    for b in range(batches):
        if b > 0:
            pre = inputs(b)
        gate = 1.0 / (1.0 + jnp.exp(-pre))
        hidden_t = (pre * gate).astype(BF)
        slope = back_ref[b] * (gate * (1.0 + pre * (1.0 - gate)))
        back_t[:, b * nodes : (b + 1) * nodes] = slope.astype(BF)
        outer_t = (nn(hidden_t, outer_sel_ref[b]) * outer_scale_ref[b]).astype(BF)
        seed_t = hidden_t[:, 0:seeds]
        logits_ref[b, :, :] = (nn(self_two_ref[...], seed_t) + nn(neigh_two_ref[...], outer_t)).T
        self_grad = nt(cot_t_ref[b], seed_t)
        neigh_grad = nt(cot_t_ref[b], outer_t)
        if b == 0:
            second[0, 0:classes, :] = self_grad
            second[1, 0:classes, :] = neigh_grad
        else:
            second[0, 0:classes, :] += self_grad
            second[1, 0:classes, :] += neigh_grad
    sent = 1 - core_ref[0]
    send_ref[0:width, :] = nt(inputs_t[sent], back_t[...]).astype(BF)
    send_ref[width:, :] = second[sent].astype(BF)


def both_passes(core, fetched, planned, self_two, neigh_two, logit_shape, half_rows):
    batches = fetched.shape[1]
    width = fetched.shape[3]
    hidden = self_two.shape[1]
    nodes = planned[0].shape[2]
    tail = half_rows - width
    return pl.pallas_call(
        pass_kernel,
        out_shape=(
            struct(logit_shape, F32),
            struct((half_rows, hidden), BF),
            struct((2, width, batches * nodes), BF),
            struct((hidden, batches * nodes), BF),
            struct((2, tail, hidden), F32),
        ),
        in_specs=[SMEM, VMEM] + [ANY] * len(planned) + [VMEM] * 2,
        out_specs=[VMEM] * 5,
        scratch_shapes=[pltpu.VMEM(value.shape, value.dtype) for value in planned]
        + [
            pltpu.VMEM((batches, width, nodes), BF),
            pltpu.SemaphoreType.DMA((len(planned) + 3 * (batches - 1),)),
        ],
        compiler_params=params(40),
        cost_estimate=cost(4_500_000_000, 20_000_000),
        name="both_passes",
    )(core, fetched, *[in_hbm(value) for value in planned], self_two, neigh_two)


def keep_kernel(core_ref, inputs_t, back_t, second, keep_ref):
    core = core_ref[0]
    width = inputs_t.shape[1]
    keep_ref[0:width, :] = nt(inputs_t[core], back_t[...])
    keep_ref[width:, :] = second[core]


def keep_half(core, inputs_t, back_t, second):
    width, nodes = inputs_t.shape[1:]
    tail, hidden = second.shape[1:]
    return pl.pallas_call(
        keep_kernel,
        out_shape=struct((width + tail, hidden), F32),
        in_specs=[SMEM] + [VMEM] * 3,
        out_specs=VMEM,
        compiler_params=params(16),
        cost_estimate=cost(2 * width * hidden * nodes, 5_000_000),
        name="keep_half",
    )(core, inputs_t, back_t, second)


def add_kernel(keep_ref, got_ref, out_ref):
    total = (keep_ref[...] + got_ref[...].astype(F32)).astype(BF)
    for j in range(out_ref.shape[0]):
        out_ref[j] = total[:, j * LANES : (j + 1) * LANES]


def add_pair(keep, got):
    return pl.pallas_call(
        add_kernel,
        out_shape=struct((keep.shape[1] // LANES, keep.shape[0], LANES), BF),
        in_specs=[VMEM] * 2,
        out_specs=VMEM,
        compiler_params=params(6),
        cost_estimate=cost(keep.size, keep.size * 8),
        name="add_pair",
    )(keep, got)


def sum_kernel(parts_ref, out_ref):
    total = parts_ref[0].astype(F32)
    for i in range(1, parts_ref.shape[0]):
        total += parts_ref[i].astype(F32)
    out_ref[...] = total.astype(BF)


def sum_parts(parts):
    return pl.pallas_call(
        sum_kernel,
        out_shape=struct(parts.shape[1:], BF),
        in_specs=[VMEM],
        out_specs=VMEM,
        compiler_params=params(3),
        cost_estimate=cost(parts.size, parts.size * 4),
        name="sum_parts",
    )(parts)


def total_kernel(own_ref, next_ref, across_ref, last_ref, out_ref):
    near = own_ref[...].astype(F32) + across_ref[...].astype(F32)
    far = next_ref[...].astype(F32) + last_ref[...].astype(F32)
    total = (near + far).astype(BF)
    for i in range(out_ref.shape[0]):
        out_ref[i] = total


def total_copies(own, got, copies):
    return pl.pallas_call(
        total_kernel,
        out_shape=struct((copies,) + own.shape, BF),
        in_specs=[VMEM] * 4,
        out_specs=VMEM,
        compiler_params=params(3),
        cost_estimate=cost(own.size * copies, own.size * copies * 2),
        name="total_copies",
    )(own, *got)


def unpack_kernel(slot_ref, half_ref, *refs):
    self_one, neigh_one, self_two, neigh_two, head, tail, sems = refs[-7:]
    width = head.shape[0]
    classes = tail.shape[0]
    parts = sems.shape[0] - 1
    block = width // parts
    columns = half_ref.shape[0]

    def place(one, two):
        copies = []
        for i in range(parts):
            here = slice(i * block, (i + 1) * block)
            for j in range(columns):
                head[here, j * LANES : (j + 1) * LANES] = half_ref[j, here, :].astype(F32)
            copies.append(pltpu.make_async_copy(head.at[here], one.at[here], sems.at[i]))
            copies[-1].start()
        for j in range(columns):
            piece = half_ref[j, width : width + classes, :].astype(F32)
            tail[:, j * LANES : (j + 1) * LANES] = piece
        copies.append(pltpu.make_async_copy(tail, two, sems.at[parts]))
        copies[-1].start()
        for copy in copies:
            copy.wait()

    @pl.when(slot_ref[0] == 0)
    def _():
        place(self_one, self_two)

    @pl.when(slot_ref[0] != 0)
    def _():
        place(neigh_one, neigh_two)


def unpack(slot, half, one_shape, two_shape, placed=()):
    return pl.pallas_call(
        unpack_kernel,
        out_shape=tuple(pltpu.HBM(shape, F32) for shape in (one_shape,) * 2 + (two_shape,) * 2),
        in_specs=[SMEM, VMEM] + [ANY] * len(placed),
        out_specs=[ANY] * 4,
        scratch_shapes=[
            pltpu.VMEM(one_shape, F32),
            pltpu.VMEM(two_shape, F32),
            pltpu.SemaphoreType.DMA((5,)),
        ],
        input_output_aliases={2 + i: i for i in range(len(placed))},
        compiler_params=params(5),
        cost_estimate=cost(half.size, half.size * 6),
        name="unpack",
    )(slot, half, *[in_hbm(value) for value in placed])


def exchange(value, axes):
    return lax.all_to_all(value, axes, split_axis=0, concat_axis=0, tiled=True)


def swap_cores(value):
    return lax.ppermute(value, "core", [(0, 1), (1, 0)])


def body(
    features, self_one, neigh_one, self_two, neigh_two, bucket_counts, request_rows,
    layer_targets, inner_slots, outer_slots, outer_degree, cotangent,
):
    batches, _, owners, capacity = request_rows.shape
    width, hidden = self_one.shape
    core = lax.axis_index("core").reshape(1).astype(jnp.int32)
    wanted = request_rows[:, 0].transpose(1, 0, 2).reshape(owners, batches * capacity)
    asked = exchange(wanted, ("chip", "core"))
    planned = plan(
        bucket_counts[:, 0],
        layer_targets,
        inner_slots.transpose(0, 2, 1),
        outer_slots.transpose(0, 2, 1),
        outer_degree,
        cotangent,
        self_one,
        neigh_one,
        self_two.T,
        neigh_two.T,
    )
    rows = serve(asked, features)
    fetched = exchange(rows.reshape(owners, batches, capacity, width), ("chip", "core"))
    plane = ("chip", "near")
    parties = lax.axis_size(plane)
    far = lax.axis_size("far")
    unit = parties * SUBLANES * LANES // hidden
    half_rows = -(-(width + cotangent.shape[2]) // unit) * unit
    logits, send, inputs_t, back_t, second = both_passes(
        core, fetched, planned, self_two.T, neigh_two.T, cotangent.shape, half_rows
    )
    got = swap_cores(send)
    half = add_pair(keep_half(core, inputs_t, back_t, second), got)
    own = sum_parts(exchange(half.reshape(parties, -1, LANES), plane))
    got = [
        lax.ppermute(own, "far", [(i, (i + shift) % far) for i in range(far)])
        for shift in range(1, far)
    ]
    mine = exchange(total_copies(own, got, parties), plane).reshape(half.shape)
    other = swap_cores(mine)
    shapes = (self_one.shape, self_two.T.shape)
    grads = unpack(1 - core, other, *shapes, unpack(core, mine, *shapes))
    return (logits, grads[0], grads[1], grads[2].T, grads[3].T)


def solution(mesh):
    stores, trainers = mesh.shape["store"], mesh.shape["trainer"]
    split = Mesh(
        mesh.devices.reshape(stores // 2, 2, trainers // 2, 2), ("chip", "core", "far", "near")
    )
    store = ("chip", "core")
    every = ("chip", "core", "far", "near")
    in_specs = (
        P(store, None),
        P(),
        P(),
        P(),
        P(),
        P(None, every, None),
        P(None, every, None, None),
        P(None, every),
        P(None, every, None),
        P(None, every, None),
        P(None, every),
        P(None, every, None),
    )
    out_specs = (P(None, every, None), P(), P(), P(), P())
    return jax.shard_map(
        body, mesh=split, in_specs=in_specs, out_specs=out_specs, check_vma=False
    )
```

```python
import jax
import jax.numpy as jnp
from jax import lax
from jax.experimental import pallas as pl
from jax.experimental.pallas import tpu as pltpu
from jax.sharding import Mesh, PartitionSpec as P

BF = jnp.bfloat16
F32 = jnp.float32
VMEM = pl.BlockSpec(memory_space=pltpu.VMEM)
SMEM = pl.BlockSpec(memory_space=pltpu.SMEM)
ANY = pl.BlockSpec(memory_space=pl.ANY)
STORE = ("y", "x", "core")
PLANE = ("x", "near", "y")
LANES = 128
SUBLANES = 8


def nn(left, right):
    return lax.dot_general(left, right, (((1,), (0,)), ((), ())), preferred_element_type=F32)


def nt(left, right):
    return lax.dot_general(left, right, (((1,), (1,)), ((), ())), preferred_element_type=F32)


def tn(left, right):
    return lax.dot_general(left, right, (((0,), (0,)), ((), ())), preferred_element_type=F32)


def struct(shape, dtype):
    return jax.ShapeDtypeStruct(shape, dtype)


def in_hbm(value):
    return pltpu.with_memory_space_constraint(value, pltpu.HBM)


def params(mebibytes):
    return pltpu.CompilerParams(vmem_limit_bytes=mebibytes * 1024 * 1024)


def cost(flops, size):
    return pl.CostEstimate(flops=flops, bytes_accessed=size, transcendentals=0)


def plan_kernel(
    counts_ref, targets_ref, inner_ref, outer_ref, degree_ref, cot_ref,
    self_one_ref, neigh_one_ref, self_two_ref, neigh_two_ref,
    own_ref, sum_ref, scale_ref, outer_sel_ref, outer_scale_ref, back_ref, self_t_ref, neigh_t_ref,
    cot_t_ref,
):
    batches, owners = counts_ref.shape
    slots, nodes = own_ref.shape[1:]
    fan_in = inner_ref.shape[1]
    fan_out, seeds = outer_ref.shape[1:]
    capacity = slots // owners
    block = 128
    self_t_ref[...] = self_one_ref[...].T
    neigh_t_ref[...] = neigh_one_ref[...].T
    for b in range(batches):
        degree = jnp.zeros((1, nodes), F32)
        for start in range(0, slots, block):
            slot = lax.broadcasted_iota(jnp.int32, (block, nodes), 0) + start
            own = jnp.where(slot == targets_ref[b : b + 1, :], 1.0, 0.0)
            own_ref[b, start : start + block, :] = own.astype(BF)
            total = jnp.zeros((block, nodes), F32)
            for k in range(fan_in):
                total += jnp.where(slot == inner_ref[b, k : k + 1, :], 1.0, 0.0)
            slot_col = lax.broadcasted_iota(jnp.int32, (block, owners), 0) + start
            owner_row = lax.broadcasted_iota(jnp.int32, (block, owners), 1)
            held = jnp.where(
                slot_col // capacity == owner_row, counts_ref[b : b + 1, :].astype(F32), 0.0
            )
            held = jnp.sum(held, axis=1, keepdims=True)
            place = lax.broadcasted_iota(jnp.int32, (block, 1), 0) % capacity
            total = jnp.where(place.astype(F32) < held, total, 0.0)
            degree += jnp.sum(total, axis=0, keepdims=True)
            sum_ref[b, start : start + block, :] = total.astype(BF)
        scale_ref[b, :, :] = 1.0 / jnp.maximum(degree, 1.0)

        seed_degree = degree_ref[b : b + 1, :]
        node = lax.broadcasted_iota(jnp.int32, (nodes, seeds), 0)
        chosen = jnp.zeros((nodes, seeds), F32)
        for k in range(fan_out):
            here = (node == outer_ref[b, k : k + 1, :]) & (seed_degree > k)
            chosen += jnp.where(here, 1.0, 0.0)
        outer_sel = chosen.astype(BF)
        outer_sel_ref[b, :, :] = outer_sel
        outer_scale = 1.0 / jnp.maximum(seed_degree.astype(F32), 1.0)
        outer_scale_ref[b, :, :] = outer_scale
        cot_t = cot_ref[b].T
        cot_t_ref[b, :, :] = cot_t
        back_seed = tn(self_two_ref[...], cot_t)
        back_mean = tn(neigh_two_ref[...], cot_t) * outer_scale
        high = back_mean.astype(BF)
        low = (back_mean - high.astype(F32)).astype(BF)
        back_ref[b, :, :] = nt(high, outer_sel) + nt(low, outer_sel)
        back_ref[b, :, 0:seeds] = back_ref[b, :, 0:seeds] + back_seed


def plan(counts, targets, inner, outer, degree, cot, self_one, neigh_one, self_two, neigh_two):
    batches, owners = counts.shape
    nodes = targets.shape[1]
    seeds, classes = cot.shape[1:]
    width, hidden = self_one.shape
    slots = nodes
    return pl.pallas_call(
        plan_kernel,
        out_shape=(
            pltpu.HBM((batches, slots, nodes), BF),
            pltpu.HBM((batches, slots, nodes), BF),
            pltpu.HBM((batches, 1, nodes), F32),
            pltpu.HBM((batches, nodes, seeds), BF),
            pltpu.HBM((batches, 1, seeds), F32),
            pltpu.HBM((batches, hidden, nodes), F32),
            pltpu.HBM((hidden, width), BF),
            pltpu.HBM((hidden, width), BF),
            pltpu.HBM((batches, classes, seeds), BF),
        ),
        in_specs=[VMEM] * 10,
        out_specs=[VMEM] * 9,
        compiler_params=params(24),
        cost_estimate=cost(200_000_000, 10_000_000),
        name="plan",
    )(counts, targets, inner, outer, degree, cot, self_one, neigh_one, self_two, neigh_two)


def serve_kernel(asked_ref, rows_ref, out_ref, landed, wide, found, sems, out_sems):
    askers, each = asked_ref.shape
    rows, width = rows_ref.shape
    chunks = sems.shape[0]
    block = rows // chunks
    pieces = width // LANES

    def load(c):
        here = pl.ds(c * block, block)
        return pltpu.make_async_copy(rows_ref.at[here, :], landed.at[here, :], sems.at[c])

    for c in range(chunks):
        load(c).start()
    for c in range(chunks):
        load(c).wait()
        for j in range(pieces):
            piece = landed[pl.ds(c * block, block), j * LANES : (j + 1) * LANES]
            wide[j, pl.ds(SUBLANES + c * block, block), :] = piece.astype(F32)

    line = lax.broadcasted_iota(jnp.int32, (SUBLANES, LANES), 0)

    def one_asker(p, carry):
        for first in range(0, each, 2 * SUBLANES):
            tiles = []
            for half in range(2):
                base = first + half * SUBLANES
                starts = [asked_ref[p, base + i] + (SUBLANES - i) for i in range(SUBLANES)]
                for j in range(pieces):
                    tile = wide[j, pl.ds(starts[0], SUBLANES), :]
                    for i in range(1, SUBLANES):
                        tile = jnp.where(line == i, wide[j, pl.ds(starts[i], SUBLANES), :], tile)
                    tiles.append(tile)
            target = pl.ds(pl.multiple_of(p * each + first, 2 * SUBLANES), 2 * SUBLANES)
            for j in range(pieces):
                pair = jnp.concatenate([tiles[j], tiles[pieces + j]], axis=0)
                found[target, j * LANES : (j + 1) * LANES] = pair.astype(BF)
        return carry

    parts = out_sems.shape[0]
    count = askers // parts
    stores = []
    for part in range(parts):
        lax.fori_loop(part * count, (part + 1) * count, one_asker, 0)
        here = pl.ds(part * count * each, count * each)
        stores.append(pltpu.make_async_copy(found.at[here, :], out_ref.at[here, :], out_sems.at[part]))
        stores[-1].start()
    for store in stores:
        store.wait()


def serve(asked, features):
    count = asked.size
    rows, width = features.shape
    chunks = 8
    return pl.pallas_call(
        serve_kernel,
        out_shape=pltpu.HBM((count, width), BF),
        in_specs=[SMEM, ANY],
        out_specs=ANY,
        scratch_shapes=[
            pltpu.VMEM((rows, width), BF),
            pltpu.VMEM((width // LANES, rows + 2 * SUBLANES, LANES), F32),
            pltpu.VMEM((count, width), BF),
            pltpu.SemaphoreType.DMA((chunks,)),
            pltpu.SemaphoreType.DMA((4,)),
        ],
        compiler_params=params(28),
        cost_estimate=cost(count * width, rows * width * 6),
        name="serve",
    )(asked, in_hbm(features))


def pass_kernel(
    core_ref, fetched_ref, own_sel_hbm, sum_sel_hbm, scale_hbm, outer_sel_hbm, outer_scale_hbm,
    back_hbm, self_t_hbm, neigh_t_hbm, cot_t_hbm, self_two_ref, neigh_two_ref,
    logits_ref, send_ref, inputs_t, back_t, second,
    own_sel_ref, sum_sel_ref, scale_ref, outer_sel_ref, outer_scale_ref, back_ref,
    self_t_ref, neigh_t_ref, cot_t_ref, table_t, sems,
):
    batches = fetched_ref.shape[1]
    slots, nodes = own_sel_ref.shape[1:]
    hidden, width = self_t_ref.shape
    seeds, classes = logits_ref.shape[1:]
    pairs = (
        (own_sel_hbm, own_sel_ref), (sum_sel_hbm, sum_sel_ref), (back_hbm, back_ref),
        (scale_hbm, scale_ref), (self_t_hbm, self_t_ref), (neigh_t_hbm, neigh_t_ref),
        (outer_sel_hbm, outer_sel_ref), (outer_scale_hbm, outer_scale_ref),
        (cot_t_hbm, cot_t_ref),
    )
    split = [
        (source.at[b], target.at[b]) for b in range(batches) for source, target in pairs[:3]
    ]
    loads = [
        pltpu.make_async_copy(source, target, sems.at[i])
        for i, (source, target) in enumerate(split + list(pairs[3:]))
    ]
    count = len(split)
    first = loads[0:2] + loads[count : count + 3]
    rest = loads[2:count] + loads[count + 3 :]
    for copy in first + rest:
        copy.start()
    second[:, classes:, :] = jnp.zeros((2, second.shape[1] - classes, hidden), F32)
    for b in range(batches):
        table_t[b] = fetched_ref[:, b].reshape(slots, width).T

    def inputs(b):
        if b == 0:
            first[0].wait()
        own_t = nn(table_t[b], own_sel_ref[b]).astype(BF)
        if b == 0:
            first[1].wait()
            first[2].wait()
        mean_t = (nn(table_t[b], sum_sel_ref[b]) * scale_ref[b]).astype(BF)
        inputs_t[0, :, b * nodes : (b + 1) * nodes] = own_t
        inputs_t[1, :, b * nodes : (b + 1) * nodes] = mean_t
        if b == 0:
            first[3].wait()
            first[4].wait()
        return nn(self_t_ref[...], own_t) + nn(neigh_t_ref[...], mean_t)

    pre = inputs(0)
    for copy in rest:
        copy.wait()
    for b in range(batches):
        if b > 0:
            pre = inputs(b)
        gate = 1.0 / (1.0 + jnp.exp(-pre))
        hidden_t = (pre * gate).astype(BF)
        slope = back_ref[b] * (gate * (1.0 + pre * (1.0 - gate)))
        back_t[:, b * nodes : (b + 1) * nodes] = slope.astype(BF)
        outer_t = (nn(hidden_t, outer_sel_ref[b]) * outer_scale_ref[b]).astype(BF)
        seed_t = hidden_t[:, 0:seeds]
        logits_ref[b, :, :] = (nn(self_two_ref[...], seed_t) + nn(neigh_two_ref[...], outer_t)).T
        self_grad = nt(cot_t_ref[b], seed_t)
        neigh_grad = nt(cot_t_ref[b], outer_t)
        if b == 0:
            second[0, 0:classes, :] = self_grad
            second[1, 0:classes, :] = neigh_grad
        else:
            second[0, 0:classes, :] += self_grad
            second[1, 0:classes, :] += neigh_grad
    sent = 1 - core_ref[0]
    send_ref[0:width, :] = nt(inputs_t[sent], back_t[...]).astype(BF)
    send_ref[width:, :] = second[sent].astype(BF)


def both_passes(core, fetched, planned, self_two, neigh_two, logit_shape, half_rows):
    batches = fetched.shape[1]
    width = fetched.shape[3]
    hidden = self_two.shape[1]
    nodes = planned[0].shape[2]
    tail = half_rows - width
    return pl.pallas_call(
        pass_kernel,
        out_shape=(
            struct(logit_shape, F32),
            struct((half_rows, hidden), BF),
            struct((2, width, batches * nodes), BF),
            struct((hidden, batches * nodes), BF),
            struct((2, tail, hidden), F32),
        ),
        in_specs=[SMEM, VMEM] + [ANY] * len(planned) + [VMEM] * 2,
        out_specs=[VMEM] * 5,
        scratch_shapes=[pltpu.VMEM(value.shape, value.dtype) for value in planned]
        + [
            pltpu.VMEM((batches, width, nodes), BF),
            pltpu.SemaphoreType.DMA((len(planned) + 3 * (batches - 1),)),
        ],
        compiler_params=params(40),
        cost_estimate=cost(4_500_000_000, 20_000_000),
        name="both_passes",
    )(core, fetched, *[in_hbm(value) for value in planned], self_two, neigh_two)


def keep_kernel(core_ref, inputs_t, back_t, second, keep_ref):
    core = core_ref[0]
    width = inputs_t.shape[1]
    keep_ref[0:width, :] = nt(inputs_t[core], back_t[...])
    keep_ref[width:, :] = second[core]


def keep_half(core, inputs_t, back_t, second):
    width, nodes = inputs_t.shape[1:]
    tail, hidden = second.shape[1:]
    return pl.pallas_call(
        keep_kernel,
        out_shape=struct((width + tail, hidden), F32),
        in_specs=[SMEM] + [VMEM] * 3,
        out_specs=VMEM,
        compiler_params=params(16),
        cost_estimate=cost(2 * width * hidden * nodes, 5_000_000),
        name="keep_half",
    )(core, inputs_t, back_t, second)


def add_kernel(keep_ref, got_ref, out_ref):
    total = (keep_ref[...] + got_ref[...].astype(F32)).astype(BF)
    for j in range(out_ref.shape[0]):
        out_ref[j] = total[:, j * LANES : (j + 1) * LANES]


def add_pair(keep, got):
    return pl.pallas_call(
        add_kernel,
        out_shape=struct((keep.shape[1] // LANES, keep.shape[0], LANES), BF),
        in_specs=[VMEM] * 2,
        out_specs=VMEM,
        compiler_params=params(6),
        cost_estimate=cost(keep.size, keep.size * 8),
        name="add_pair",
    )(keep, got)


def sum_kernel(parts_ref, out_ref):
    total = parts_ref[0].astype(F32)
    for i in range(1, parts_ref.shape[0]):
        total += parts_ref[i].astype(F32)
    out_ref[...] = total.astype(BF)


def sum_parts(parts):
    return pl.pallas_call(
        sum_kernel,
        out_shape=struct(parts.shape[1:], BF),
        in_specs=[VMEM],
        out_specs=VMEM,
        compiler_params=params(3),
        cost_estimate=cost(parts.size, parts.size * 4),
        name="sum_parts",
    )(parts)


def total_kernel(own_ref, next_ref, across_ref, last_ref, out_ref):
    near = own_ref[...].astype(F32) + across_ref[...].astype(F32)
    far = next_ref[...].astype(F32) + last_ref[...].astype(F32)
    total = (near + far).astype(BF)
    for i in range(out_ref.shape[0]):
        out_ref[i] = total


def total_copies(own, got, copies):
    return pl.pallas_call(
        total_kernel,
        out_shape=struct((copies,) + own.shape, BF),
        in_specs=[VMEM] * 4,
        out_specs=VMEM,
        compiler_params=params(3),
        cost_estimate=cost(own.size * copies, own.size * copies * 2),
        name="total_copies",
    )(own, *got)


def unpack_kernel(slot_ref, half_ref, *refs):
    self_one, neigh_one, self_two, neigh_two, head, tail, sems = refs[-7:]
    width = head.shape[0]
    classes = tail.shape[0]
    parts = sems.shape[0] - 1
    block = width // parts
    columns = half_ref.shape[0]

    def place(one, two):
        copies = []
        for i in range(parts):
            here = slice(i * block, (i + 1) * block)
            for j in range(columns):
                head[here, j * LANES : (j + 1) * LANES] = half_ref[j, here, :].astype(F32)
            copies.append(pltpu.make_async_copy(head.at[here], one.at[here], sems.at[i]))
            copies[-1].start()
        for j in range(columns):
            piece = half_ref[j, width : width + classes, :].astype(F32)
            tail[:, j * LANES : (j + 1) * LANES] = piece
        copies.append(pltpu.make_async_copy(tail, two, sems.at[parts]))
        copies[-1].start()
        for copy in copies:
            copy.wait()

    @pl.when(slot_ref[0] == 0)
    def _():
        place(self_one, self_two)

    @pl.when(slot_ref[0] != 0)
    def _():
        place(neigh_one, neigh_two)


def unpack(slot, half, one_shape, two_shape, placed=()):
    return pl.pallas_call(
        unpack_kernel,
        out_shape=tuple(pltpu.HBM(shape, F32) for shape in (one_shape,) * 2 + (two_shape,) * 2),
        in_specs=[SMEM, VMEM] + [ANY] * len(placed),
        out_specs=[ANY] * 4,
        scratch_shapes=[
            pltpu.VMEM(one_shape, F32),
            pltpu.VMEM(two_shape, F32),
            pltpu.SemaphoreType.DMA((5,)),
        ],
        input_output_aliases={2 + i: i for i in range(len(placed))},
        compiler_params=params(5),
        cost_estimate=cost(half.size, half.size * 6),
        name="unpack",
    )(slot, half, *[in_hbm(value) for value in placed])


def exchange(value, axes):
    return lax.all_to_all(value, axes, split_axis=0, concat_axis=0, tiled=True)


def swap_cores(value):
    return lax.ppermute(value, "core", [(0, 1), (1, 0)])


def body(
    features, self_one, neigh_one, self_two, neigh_two, bucket_counts, request_rows,
    layer_targets, inner_slots, outer_slots, outer_degree, cotangent,
):
    batches, _, owners, capacity = request_rows.shape
    width, hidden = self_one.shape
    core = lax.axis_index("core").reshape(1).astype(jnp.int32)
    wanted = request_rows[:, 0].transpose(1, 0, 2).reshape(owners, batches * capacity)
    asked = exchange(wanted, STORE)
    planned = plan(
        bucket_counts[:, 0],
        layer_targets,
        inner_slots.transpose(0, 2, 1),
        outer_slots.transpose(0, 2, 1),
        outer_degree,
        cotangent,
        self_one,
        neigh_one,
        self_two.T,
        neigh_two.T,
    )
    rows = serve(asked, features)
    fetched = exchange(rows.reshape(owners, batches, capacity, width), STORE)
    plane = PLANE
    parties = lax.axis_size(plane)
    far = lax.axis_size("far")
    unit = parties * SUBLANES * LANES // hidden
    half_rows = -(-(width + cotangent.shape[2]) // unit) * unit
    logits, send, inputs_t, back_t, second = both_passes(
        core, fetched, planned, self_two.T, neigh_two.T, cotangent.shape, half_rows
    )
    got = swap_cores(send)
    half = add_pair(keep_half(core, inputs_t, back_t, second), got)
    own = sum_parts(exchange(half.reshape(parties, -1, LANES), plane))
    got = [
        lax.ppermute(own, "far", [(i, (i + shift) % far) for i in range(far)])
        for shift in range(1, far)
    ]
    mine = exchange(total_copies(own, got, parties), plane).reshape(half.shape)
    other = swap_cores(mine)
    shapes = (self_one.shape, self_two.T.shape)
    grads = unpack(1 - core, other, *shapes, unpack(core, mine, *shapes))
    return (logits, grads[0], grads[1], grads[2].T, grads[3].T)


def solution(mesh):
    stores, trainers = mesh.shape["store"], mesh.shape["trainer"]
    chips = stores // 2
    side = int(chips**0.5)
    split = Mesh(
        mesh.devices.reshape(chips // side, side, 2, trainers // 2, 2), STORE + ("far", "near")
    )
    every = STORE + ("far", "near")
    in_specs = (
        P(STORE, None),
        P(),
        P(),
        P(),
        P(),
        P(None, every, None),
        P(None, every, None, None),
        P(None, every),
        P(None, every, None),
        P(None, every, None),
        P(None, every),
        P(None, every, None),
    )
    out_specs = (P(None, every, None), P(), P(), P(), P())
    return jax.shard_map(
        body, mesh=split, in_specs=in_specs, out_specs=out_specs, check_vma=False
    )
```

```python
import functools

import jax
import jax.numpy as jnp
from jax import lax
from jax.experimental import pallas as pl
from jax.experimental.pallas import tpu as pltpu
from jax.sharding import Mesh, PartitionSpec as P

BF = jnp.bfloat16
F32 = jnp.float32
VMEM = pl.BlockSpec(memory_space=pltpu.VMEM)
SMEM = pl.BlockSpec(memory_space=pltpu.SMEM)
ANY = pl.BlockSpec(memory_space=pl.ANY)
STORE = ("y", "x", "core")
PLANE = ("x", "near", "y")
LANES = 128
SUBLANES = 8


def nn(left, right):
    return lax.dot_general(left, right, (((1,), (0,)), ((), ())), preferred_element_type=F32)


def nt(left, right):
    return lax.dot_general(left, right, (((1,), (1,)), ((), ())), preferred_element_type=F32)


def tn(left, right):
    return lax.dot_general(left, right, (((0,), (0,)), ((), ())), preferred_element_type=F32)


def struct(shape, dtype):
    return jax.ShapeDtypeStruct(shape, dtype)


def in_hbm(value):
    return pltpu.with_memory_space_constraint(value, pltpu.HBM)


def params(mebibytes):
    return pltpu.CompilerParams(vmem_limit_bytes=mebibytes * 1024 * 1024)


def cost(flops, size):
    return pl.CostEstimate(flops=flops, bytes_accessed=size, transcendentals=0)


def plan_kernel(
    counts_ref, targets_ref, inner_ref, outer_ref, degree_ref, cot_ref,
    self_one_ref, neigh_one_ref, self_two_ref, neigh_two_ref,
    own_ref, sum_ref, scale_ref, outer_sel_ref, outer_scale_ref, back_ref, self_t_ref, neigh_t_ref,
    cot_t_ref,
):
    batches, owners = counts_ref.shape
    slots, nodes = own_ref.shape[1:]
    fan_in = inner_ref.shape[1]
    fan_out, seeds = outer_ref.shape[1:]
    capacity = slots // owners
    block = 128
    self_t_ref[...] = self_one_ref[...].T
    neigh_t_ref[...] = neigh_one_ref[...].T
    for b in range(batches):
        degree = jnp.zeros((1, nodes), F32)
        for start in range(0, slots, block):
            slot = lax.broadcasted_iota(jnp.int32, (block, nodes), 0) + start
            own = jnp.where(slot == targets_ref[b : b + 1, :], 1.0, 0.0)
            own_ref[b, start : start + block, :] = own.astype(BF)
            total = jnp.zeros((block, nodes), F32)
            for k in range(fan_in):
                total += jnp.where(slot == inner_ref[b, k : k + 1, :], 1.0, 0.0)
            slot_col = lax.broadcasted_iota(jnp.int32, (block, owners), 0) + start
            owner_row = lax.broadcasted_iota(jnp.int32, (block, owners), 1)
            held = jnp.where(
                slot_col // capacity == owner_row, counts_ref[b : b + 1, :].astype(F32), 0.0
            )
            held = jnp.sum(held, axis=1, keepdims=True)
            place = lax.broadcasted_iota(jnp.int32, (block, 1), 0) % capacity
            total = jnp.where(place.astype(F32) < held, total, 0.0)
            degree += jnp.sum(total, axis=0, keepdims=True)
            sum_ref[b, start : start + block, :] = total.astype(BF)
        scale_ref[b, :, :] = 1.0 / jnp.maximum(degree, 1.0)

        seed_degree = degree_ref[b : b + 1, :]
        node = lax.broadcasted_iota(jnp.int32, (nodes, seeds), 0)
        chosen = jnp.zeros((nodes, seeds), F32)
        for k in range(fan_out):
            here = (node == outer_ref[b, k : k + 1, :]) & (seed_degree > k)
            chosen += jnp.where(here, 1.0, 0.0)
        outer_sel = chosen.astype(BF)
        outer_sel_ref[b, :, :] = outer_sel
        outer_scale = 1.0 / jnp.maximum(seed_degree.astype(F32), 1.0)
        outer_scale_ref[b, :, :] = outer_scale
        cot_t = cot_ref[b].T
        cot_t_ref[b, :, :] = cot_t
        back_seed = tn(self_two_ref[...], cot_t)
        back_mean = tn(neigh_two_ref[...], cot_t) * outer_scale
        high = back_mean.astype(BF)
        low = (back_mean - high.astype(F32)).astype(BF)
        back_ref[b, :, :] = nt(high, outer_sel) + nt(low, outer_sel)
        back_ref[b, :, 0:seeds] = back_ref[b, :, 0:seeds] + back_seed


def plan(counts, targets, inner, outer, degree, cot, self_one, neigh_one, self_two, neigh_two):
    batches, owners = counts.shape
    nodes = targets.shape[1]
    seeds, classes = cot.shape[1:]
    width, hidden = self_one.shape
    slots = nodes
    return pl.pallas_call(
        plan_kernel,
        out_shape=(
            pltpu.HBM((batches, slots, nodes), BF),
            pltpu.HBM((batches, slots, nodes), BF),
            pltpu.HBM((batches, 1, nodes), F32),
            pltpu.HBM((batches, nodes, seeds), BF),
            pltpu.HBM((batches, 1, seeds), F32),
            pltpu.HBM((batches, hidden, nodes), F32),
            pltpu.HBM((hidden, width), BF),
            pltpu.HBM((hidden, width), BF),
            pltpu.HBM((batches, classes, seeds), BF),
        ),
        in_specs=[VMEM] * 10,
        out_specs=[VMEM] * 9,
        compiler_params=params(24),
        cost_estimate=cost(200_000_000, 10_000_000),
        name="plan",
    )(counts, targets, inner, outer, degree, cot, self_one, neigh_one, self_two, neigh_two)


def serve_kernel(
    asked_any, rows_ref, out_ref, asked_ref, landed, wide, found, sems, out_sems, asked_sem
):
    askers, each = asked_ref.shape
    rows, width = rows_ref.shape
    chunks = sems.shape[0]
    block = rows // chunks
    pieces = width // LANES

    def load(c):
        here = pl.ds(c * block, block)
        return pltpu.make_async_copy(rows_ref.at[here, :], landed.at[here, :], sems.at[c])

    asked_load = pltpu.make_async_copy(asked_any, asked_ref, asked_sem)
    for c in range(chunks):
        load(c).start()
    asked_load.start()
    for c in range(chunks):
        load(c).wait()
        for j in range(pieces):
            piece = landed[pl.ds(c * block, block), j * LANES : (j + 1) * LANES]
            wide[j, pl.ds(SUBLANES + c * block, block), :] = piece.astype(F32)

    asked_load.wait()
    line = lax.broadcasted_iota(jnp.int32, (SUBLANES, LANES), 0)

    def one_asker(p, carry):
        for first in range(0, each, 2 * SUBLANES):
            tiles = []
            for half in range(2):
                base = first + half * SUBLANES
                starts = [asked_ref[p, base + i] + (SUBLANES - i) for i in range(SUBLANES)]
                for j in range(pieces):
                    tile = wide[j, pl.ds(starts[0], SUBLANES), :]
                    for i in range(1, SUBLANES):
                        tile = jnp.where(line == i, wide[j, pl.ds(starts[i], SUBLANES), :], tile)
                    tiles.append(tile)
            target = pl.ds(pl.multiple_of(p * each + first, 2 * SUBLANES), 2 * SUBLANES)
            for j in range(pieces):
                pair = jnp.concatenate([tiles[j], tiles[pieces + j]], axis=0)
                found[target, j * LANES : (j + 1) * LANES] = pair.astype(BF)
        return carry

    parts = out_sems.shape[0]
    count = askers // parts
    stores = []
    for part in range(parts):
        lax.fori_loop(part * count, (part + 1) * count, one_asker, 0)
        here = pl.ds(part * count * each, count * each)
        stores.append(pltpu.make_async_copy(found.at[here, :], out_ref.at[here, :], out_sems.at[part]))
        stores[-1].start()
    for store in stores:
        store.wait()


def serve(asked, features):
    count = asked.size
    rows, width = features.shape
    chunks = 8
    return pl.pallas_call(
        serve_kernel,
        out_shape=pltpu.HBM((count, width), BF),
        in_specs=[ANY, ANY],
        out_specs=ANY,
        scratch_shapes=[
            pltpu.SMEM(asked.shape, asked.dtype),
            pltpu.VMEM((rows, width), BF),
            pltpu.VMEM((width // LANES, rows + 2 * SUBLANES, LANES), F32),
            pltpu.VMEM((count, width), BF),
            pltpu.SemaphoreType.DMA((chunks,)),
            pltpu.SemaphoreType.DMA((4,)),
            pltpu.SemaphoreType.DMA,
        ],
        compiler_params=params(28),
        cost_estimate=cost(count * width, rows * width * 6),
        name="serve",
    )(asked, in_hbm(features))


def pass_kernel(
    fetched_ref, own_sel_hbm, sum_sel_hbm, scale_hbm, outer_sel_hbm, outer_scale_hbm,
    back_hbm, self_t_hbm, neigh_t_hbm, cot_t_hbm, self_two_hbm, neigh_two_hbm,
    logits_ref, send_ref, inputs_t, back_t, second,
    own_sel_ref, sum_sel_ref, scale_ref, outer_sel_ref, outer_scale_ref, back_ref,
    self_t_ref, neigh_t_ref, cot_t_ref, self_two_ref, neigh_two_ref, table_t, sems,
):
    batches = fetched_ref.shape[1]
    slots, nodes = own_sel_ref.shape[1:]
    hidden, width = self_t_ref.shape
    seeds, classes = logits_ref.shape[1:]
    pairs = (
        (own_sel_hbm, own_sel_ref), (sum_sel_hbm, sum_sel_ref), (back_hbm, back_ref),
        (scale_hbm, scale_ref), (self_t_hbm, self_t_ref), (neigh_t_hbm, neigh_t_ref),
        (outer_sel_hbm, outer_sel_ref), (outer_scale_hbm, outer_scale_ref),
        (cot_t_hbm, cot_t_ref), (self_two_hbm, self_two_ref), (neigh_two_hbm, neigh_two_ref),
    )
    split = [
        (source.at[b], target.at[b]) for b in range(batches) for source, target in pairs[:3]
    ]
    loads = [
        pltpu.make_async_copy(source, target, sems.at[i])
        for i, (source, target) in enumerate(split + list(pairs[3:]))
    ]
    count = len(split)
    first = loads[0:2] + loads[count : count + 3]
    rest = loads[2:count] + loads[count + 3 :]
    for copy in first + rest:
        copy.start()
    second[:, classes:, :] = jnp.zeros((2, second.shape[1] - classes, hidden), F32)
    for b in range(batches):
        table_t[b] = fetched_ref[:, b].reshape(slots, width).T

    def inputs(b):
        if b == 0:
            first[0].wait()
        own_t = nn(table_t[b], own_sel_ref[b]).astype(BF)
        if b == 0:
            first[1].wait()
            first[2].wait()
        mean_t = (nn(table_t[b], sum_sel_ref[b]) * scale_ref[b]).astype(BF)
        inputs_t[0, :, b * nodes : (b + 1) * nodes] = own_t
        inputs_t[1, :, b * nodes : (b + 1) * nodes] = mean_t
        if b == 0:
            first[3].wait()
            first[4].wait()
        return nn(self_t_ref[...], own_t) + nn(neigh_t_ref[...], mean_t)

    pre = inputs(0)
    for copy in rest:
        copy.wait()
    for b in range(batches):
        if b > 0:
            pre = inputs(b)
        gate = 1.0 / (1.0 + jnp.exp(-pre))
        hidden_t = (pre * gate).astype(BF)
        slope = back_ref[b] * (gate * (1.0 + pre * (1.0 - gate)))
        back_t[:, b * nodes : (b + 1) * nodes] = slope.astype(BF)
        outer_t = (nn(hidden_t, outer_sel_ref[b]) * outer_scale_ref[b]).astype(BF)
        seed_t = hidden_t[:, 0:seeds]
        logits_ref[b, :, :] = (nn(self_two_ref[...], seed_t) + nn(neigh_two_ref[...], outer_t)).T
        self_grad = nt(cot_t_ref[b], seed_t)
        neigh_grad = nt(cot_t_ref[b], outer_t)
        if b == 0:
            second[0, 0:classes, :] = self_grad
            second[1, 0:classes, :] = neigh_grad
        else:
            second[0, 0:classes, :] += self_grad
            second[1, 0:classes, :] += neigh_grad
    sent = 1 - lax.axis_index("core")
    send_ref[0:width, :] = nt(inputs_t[sent], back_t[...]).astype(BF)
    send_ref[width:, :] = second[sent].astype(BF)


def both_passes(fetched, planned, self_two, neigh_two, logit_shape, half_rows):
    batches = fetched.shape[1]
    width = fetched.shape[3]
    hidden = self_two.shape[1]
    nodes = planned[0].shape[2]
    tail = half_rows - width
    loaded = (*planned, self_two, neigh_two)
    return pl.pallas_call(
        pass_kernel,
        out_shape=(
            struct(logit_shape, F32),
            struct((half_rows, hidden), BF),
            struct((2, width, batches * nodes), BF),
            struct((hidden, batches * nodes), BF),
            struct((2, tail, hidden), F32),
        ),
        in_specs=[VMEM] + [ANY] * len(loaded),
        out_specs=[VMEM] * 5,
        scratch_shapes=[pltpu.VMEM(value.shape, value.dtype) for value in loaded]
        + [
            pltpu.VMEM((batches, width, nodes), BF),
            pltpu.SemaphoreType.DMA((len(loaded) + 3 * (batches - 1),)),
        ],
        compiler_params=params(40),
        cost_estimate=cost(4_500_000_000, 20_000_000),
        name="both_passes",
    )(fetched, *[in_hbm(value) for value in loaded])


def keep_kernel(inputs_t, back_t, second, keep_ref):
    core = lax.axis_index("core")
    width = inputs_t.shape[1]
    keep_ref[0:width, :] = nt(inputs_t[core], back_t[...])
    keep_ref[width:, :] = second[core]


def keep_half(inputs_t, back_t, second):
    width, nodes = inputs_t.shape[1:]
    tail, hidden = second.shape[1:]
    return pl.pallas_call(
        keep_kernel,
        out_shape=struct((width + tail, hidden), F32),
        in_specs=[VMEM] * 3,
        out_specs=VMEM,
        compiler_params=params(16),
        cost_estimate=cost(2 * width * hidden * nodes, 5_000_000),
        name="keep_half",
    )(inputs_t, back_t, second)


def add_kernel(keep_ref, got_ref, out_ref):
    total = (keep_ref[...] + got_ref[...].astype(F32)).astype(BF)
    for j in range(out_ref.shape[0]):
        out_ref[j] = total[:, j * LANES : (j + 1) * LANES]


def add_pair(keep, got):
    return pl.pallas_call(
        add_kernel,
        out_shape=struct((keep.shape[1] // LANES, keep.shape[0], LANES), BF),
        in_specs=[VMEM] * 2,
        out_specs=VMEM,
        compiler_params=params(6),
        cost_estimate=cost(keep.size, keep.size * 8),
        name="add_pair",
    )(keep, got)


def sum_kernel(parts_ref, out_ref):
    total = parts_ref[0].astype(F32)
    for i in range(1, parts_ref.shape[0]):
        total += parts_ref[i].astype(F32)
    out_ref[...] = total.astype(BF)


def sum_parts(parts):
    return pl.pallas_call(
        sum_kernel,
        out_shape=struct(parts.shape[1:], BF),
        in_specs=[VMEM],
        out_specs=VMEM,
        compiler_params=params(3),
        cost_estimate=cost(parts.size, parts.size * 4),
        name="sum_parts",
    )(parts)


def total_kernel(own_ref, next_ref, across_ref, last_ref, out_ref):
    near = own_ref[...].astype(F32) + across_ref[...].astype(F32)
    far = next_ref[...].astype(F32) + last_ref[...].astype(F32)
    total = (near + far).astype(BF)
    for i in range(out_ref.shape[0]):
        out_ref[i] = total


def total_copies(own, got, copies):
    return pl.pallas_call(
        total_kernel,
        out_shape=struct((copies,) + own.shape, BF),
        in_specs=[VMEM] * 4,
        out_specs=VMEM,
        compiler_params=params(3),
        cost_estimate=cost(own.size * copies, own.size * copies * 2),
        name="total_copies",
    )(own, *got)


def unpack_kernel(mine, half_ref, *refs):
    self_one, neigh_one, self_two, neigh_two, head, tail, sems = refs[-7:]
    width = head.shape[0]
    classes = tail.shape[0]
    parts = sems.shape[0] - 1
    block = width // parts
    columns = half_ref.shape[0]

    def place(one, two):
        copies = []
        for i in range(parts):
            here = slice(i * block, (i + 1) * block)
            for j in range(columns):
                head[here, j * LANES : (j + 1) * LANES] = half_ref[j, here, :].astype(F32)
            copies.append(pltpu.make_async_copy(head.at[here], one.at[here], sems.at[i]))
            copies[-1].start()
        for j in range(columns):
            piece = half_ref[j, width : width + classes, :].astype(F32)
            tail[:, j * LANES : (j + 1) * LANES] = piece
        copies.append(pltpu.make_async_copy(tail, two, sems.at[parts]))
        copies[-1].start()
        for copy in copies:
            copy.wait()

    core = lax.axis_index("core")
    slot = core if mine else 1 - core

    @pl.when(slot == 0)
    def _():
        place(self_one, self_two)

    @pl.when(slot != 0)
    def _():
        place(neigh_one, neigh_two)


def unpack(mine, half, one_shape, two_shape, placed=()):
    return pl.pallas_call(
        functools.partial(unpack_kernel, mine),
        out_shape=tuple(pltpu.HBM(shape, F32) for shape in (one_shape,) * 2 + (two_shape,) * 2),
        in_specs=[VMEM] + [ANY] * len(placed),
        out_specs=[ANY] * 4,
        scratch_shapes=[
            pltpu.VMEM(one_shape, F32),
            pltpu.VMEM(two_shape, F32),
            pltpu.SemaphoreType.DMA((5,)),
        ],
        input_output_aliases={1 + i: i for i in range(len(placed))},
        compiler_params=params(5),
        cost_estimate=cost(half.size, half.size * 6),
        name="unpack",
    )(half, *[in_hbm(value) for value in placed])


def exchange(value, axes):
    return lax.all_to_all(value, axes, split_axis=0, concat_axis=0, tiled=True)


def swap_cores(value):
    return lax.ppermute(value, "core", [(0, 1), (1, 0)])


def body(
    features, self_one, neigh_one, self_two, neigh_two, bucket_counts, request_rows,
    layer_targets, inner_slots, outer_slots, outer_degree, cotangent,
):
    batches, _, owners, capacity = request_rows.shape
    width, hidden = self_one.shape
    wanted = request_rows[:, 0].transpose(1, 0, 2).reshape(owners, batches * capacity)
    asked = exchange(wanted, STORE)
    planned = plan(
        bucket_counts[:, 0],
        layer_targets,
        inner_slots.transpose(0, 2, 1),
        outer_slots.transpose(0, 2, 1),
        outer_degree,
        cotangent,
        self_one,
        neigh_one,
        self_two.T,
        neigh_two.T,
    )
    rows = serve(asked, features)
    fetched = exchange(rows.reshape(owners, batches, capacity, width), STORE)
    plane = PLANE
    parties = lax.axis_size(plane)
    far = lax.axis_size("far")
    unit = parties * SUBLANES * LANES // hidden
    half_rows = -(-(width + cotangent.shape[2]) // unit) * unit
    logits, send, inputs_t, back_t, second = both_passes(
        fetched, planned, self_two.T, neigh_two.T, cotangent.shape, half_rows
    )
    got = swap_cores(send)
    half = add_pair(keep_half(inputs_t, back_t, second), got)
    own = sum_parts(exchange(half.reshape(parties, -1, LANES), plane))
    got = [
        lax.ppermute(own, "far", [(i, (i + shift) % far) for i in range(far)])
        for shift in range(1, far)
    ]
    mine = exchange(total_copies(own, got, parties), plane).reshape(half.shape)
    other = swap_cores(mine)
    shapes = (self_one.shape, self_two.T.shape)
    grads = unpack(False, other, *shapes, unpack(True, mine, *shapes))
    return (logits, grads[0], grads[1], grads[2].T, grads[3].T)


def solution(mesh):
    stores, trainers = mesh.shape["store"], mesh.shape["trainer"]
    chips = stores // 2
    side = int(chips**0.5)
    split = Mesh(
        mesh.devices.reshape(chips // side, side, 2, trainers // 2, 2), STORE + ("far", "near")
    )
    every = STORE + ("far", "near")
    in_specs = (
        P(STORE, None),
        P(),
        P(),
        P(),
        P(),
        P(None, every, None),
        P(None, every, None, None),
        P(None, every),
        P(None, every, None),
        P(None, every, None),
        P(None, every),
        P(None, every, None),
    )
    out_specs = (P(None, every, None), P(), P(), P(), P())
    return jax.shard_map(
        body, mesh=split, in_specs=in_specs, out_specs=out_specs, check_vma=False
    )
```

```python
import functools

import jax
import jax.numpy as jnp
from jax import lax
from jax.experimental import pallas as pl
from jax.experimental.pallas import tpu as pltpu
from jax.sharding import Mesh, PartitionSpec as P

BF = jnp.bfloat16
F32 = jnp.float32
VMEM = pl.BlockSpec(memory_space=pltpu.VMEM)
SMEM = pl.BlockSpec(memory_space=pltpu.SMEM)
ANY = pl.BlockSpec(memory_space=pl.ANY)
STORE = ("y", "x", "core")
PLANE = ("x", "near", "y")
LANES = 128
SUBLANES = 8


def nn(left, right):
    return lax.dot_general(left, right, (((1,), (0,)), ((), ())), preferred_element_type=F32)


def nt(left, right):
    return lax.dot_general(left, right, (((1,), (1,)), ((), ())), preferred_element_type=F32)


def tn(left, right):
    return lax.dot_general(left, right, (((0,), (0,)), ((), ())), preferred_element_type=F32)


def struct(shape, dtype):
    return jax.ShapeDtypeStruct(shape, dtype)


def in_hbm(value):
    return pltpu.with_memory_space_constraint(value, pltpu.HBM)


def params(mebibytes):
    return pltpu.CompilerParams(vmem_limit_bytes=mebibytes * 1024 * 1024)


def cost(flops, size):
    return pl.CostEstimate(flops=flops, bytes_accessed=size, transcendentals=0)


def plan_kernel(
    counts_ref, targets_ref, inner_ref, outer_ref, degree_ref, cot_ref,
    self_one_ref, neigh_one_ref, self_two_ref, neigh_two_ref,
    own_ref, sum_ref, scale_ref, outer_sel_ref, outer_scale_ref, back_ref, self_t_ref, neigh_t_ref,
    cot_t_ref,
):
    batches, owners = counts_ref.shape
    slots, nodes = own_ref.shape[1:]
    fan_in = inner_ref.shape[1]
    fan_out, seeds = outer_ref.shape[1:]
    capacity = slots // owners
    block = 128
    self_t_ref[...] = self_one_ref[...].T
    neigh_t_ref[...] = neigh_one_ref[...].T
    for b in range(batches):
        degree = jnp.zeros((1, nodes), F32)
        for start in range(0, slots, block):
            slot = lax.broadcasted_iota(jnp.int32, (block, nodes), 0) + start
            own = jnp.where(slot == targets_ref[b : b + 1, :], 1.0, 0.0)
            own_ref[b, start : start + block, :] = own.astype(BF)
            total = jnp.zeros((block, nodes), F32)
            for k in range(fan_in):
                total += jnp.where(slot == inner_ref[b, k : k + 1, :], 1.0, 0.0)
            slot_col = lax.broadcasted_iota(jnp.int32, (block, owners), 0) + start
            owner_row = lax.broadcasted_iota(jnp.int32, (block, owners), 1)
            held = jnp.where(
                slot_col // capacity == owner_row, counts_ref[b : b + 1, :].astype(F32), 0.0
            )
            held = jnp.sum(held, axis=1, keepdims=True)
            place = lax.broadcasted_iota(jnp.int32, (block, 1), 0) % capacity
            total = jnp.where(place.astype(F32) < held, total, 0.0)
            degree += jnp.sum(total, axis=0, keepdims=True)
            sum_ref[b, start : start + block, :] = total.astype(BF)
        scale_ref[b, :, :] = 1.0 / jnp.maximum(degree, 1.0)

        seed_degree = degree_ref[b : b + 1, :]
        node = lax.broadcasted_iota(jnp.int32, (nodes, seeds), 0)
        chosen = jnp.zeros((nodes, seeds), F32)
        for k in range(fan_out):
            here = (node == outer_ref[b, k : k + 1, :]) & (seed_degree > k)
            chosen += jnp.where(here, 1.0, 0.0)
        outer_sel = chosen.astype(BF)
        outer_sel_ref[b, :, :] = outer_sel
        outer_scale = 1.0 / jnp.maximum(seed_degree.astype(F32), 1.0)
        outer_scale_ref[b, :, :] = outer_scale
        cot_t = cot_ref[b].T
        cot_t_ref[b, :, :] = cot_t
        back_seed = tn(self_two_ref[...], cot_t)
        back_mean = tn(neigh_two_ref[...], cot_t) * outer_scale
        high = back_mean.astype(BF)
        low = (back_mean - high.astype(F32)).astype(BF)
        back_ref[b, :, :] = nt(high, outer_sel) + nt(low, outer_sel)
        back_ref[b, :, 0:seeds] = back_ref[b, :, 0:seeds] + back_seed


def plan(counts, targets, inner, outer, degree, cot, self_one, neigh_one, self_two, neigh_two):
    batches, owners = counts.shape
    nodes = targets.shape[1]
    seeds, classes = cot.shape[1:]
    width, hidden = self_one.shape
    slots = nodes
    return pl.pallas_call(
        plan_kernel,
        out_shape=(
            pltpu.HBM((batches, slots, nodes), BF),
            pltpu.HBM((batches, slots, nodes), BF),
            pltpu.HBM((batches, 1, nodes), F32),
            pltpu.HBM((batches, nodes, seeds), BF),
            pltpu.HBM((batches, 1, seeds), F32),
            pltpu.HBM((batches, hidden, nodes), F32),
            pltpu.HBM((hidden, width), BF),
            pltpu.HBM((hidden, width), BF),
            pltpu.HBM((batches, classes, seeds), BF),
        ),
        in_specs=[VMEM] * 10,
        out_specs=[VMEM] * 9,
        compiler_params=params(24),
        cost_estimate=cost(200_000_000, 10_000_000),
        name="plan",
    )(counts, targets, inner, outer, degree, cot, self_one, neigh_one, self_two, neigh_two)


def serve_kernel(
    asked_any, rows_ref, out_ref, asked_ref, landed, wide, found, sems, out_sems, asked_sem
):
    askers, each = asked_ref.shape
    rows, width = rows_ref.shape
    chunks = sems.shape[0]
    block = rows // chunks
    pieces = width // LANES

    def load(c):
        here = pl.ds(c * block, block)
        return pltpu.make_async_copy(rows_ref.at[here, :], landed.at[here, :], sems.at[c])

    asked_load = pltpu.make_async_copy(asked_any, asked_ref, asked_sem)
    for c in range(chunks):
        load(c).start()
    asked_load.start()
    for c in range(chunks):
        load(c).wait()
        for j in range(pieces):
            piece = landed[pl.ds(c * block, block), j * LANES : (j + 1) * LANES]
            wide[j, pl.ds(SUBLANES + c * block, block), :] = piece.astype(F32)

    asked_load.wait()
    line = lax.broadcasted_iota(jnp.int32, (SUBLANES, LANES), 0)

    def one_asker(p, carry):
        for first in range(0, each, 2 * SUBLANES):
            tiles = []
            for half in range(2):
                base = first + half * SUBLANES
                starts = [asked_ref[p, base + i] + (SUBLANES - i) for i in range(SUBLANES)]
                for j in range(pieces):
                    tile = wide[j, pl.ds(starts[0], SUBLANES), :]
                    for i in range(1, SUBLANES):
                        tile = jnp.where(line == i, wide[j, pl.ds(starts[i], SUBLANES), :], tile)
                    tiles.append(tile)
            target = pl.ds(pl.multiple_of(p * each + first, 2 * SUBLANES), 2 * SUBLANES)
            for j in range(pieces):
                pair = jnp.concatenate([tiles[j], tiles[pieces + j]], axis=0)
                found[target, j * LANES : (j + 1) * LANES] = pair.astype(BF)
        return carry

    parts = out_sems.shape[0]
    count = askers // parts
    stores = []
    for part in range(parts):
        lax.fori_loop(part * count, (part + 1) * count, one_asker, 0)
        here = pl.ds(part * count * each, count * each)
        stores.append(pltpu.make_async_copy(found.at[here, :], out_ref.at[here, :], out_sems.at[part]))
        stores[-1].start()
    for store in stores:
        store.wait()


def serve(asked, features):
    count = asked.size
    rows, width = features.shape
    chunks = 8
    return pl.pallas_call(
        serve_kernel,
        out_shape=pltpu.HBM((count, width), BF),
        in_specs=[ANY, ANY],
        out_specs=ANY,
        scratch_shapes=[
            pltpu.SMEM(asked.shape, asked.dtype),
            pltpu.VMEM((rows, width), BF),
            pltpu.VMEM((width // LANES, rows + 2 * SUBLANES, LANES), F32),
            pltpu.VMEM((count, width), BF),
            pltpu.SemaphoreType.DMA((chunks,)),
            pltpu.SemaphoreType.DMA((4,)),
            pltpu.SemaphoreType.DMA,
        ],
        compiler_params=params(28),
        cost_estimate=cost(count * width, rows * width * 6),
        name="serve",
    )(asked, in_hbm(features))


def pass_kernel(
    fetched_ref, own_sel_hbm, sum_sel_hbm, scale_hbm, outer_sel_hbm, outer_scale_hbm,
    back_hbm, self_t_hbm, neigh_t_hbm, cot_t_hbm,
    seeds_t, send_ref, inputs_t, back_t, second,
    own_sel_ref, sum_sel_ref, scale_ref, outer_sel_ref, outer_scale_ref, back_ref,
    self_t_ref, neigh_t_ref, cot_t_ref, table_t, sems,
):
    batches = fetched_ref.shape[1]
    slots, nodes = own_sel_ref.shape[1:]
    hidden, width = self_t_ref.shape
    classes, seeds = cot_t_ref.shape[1:]
    pairs = (
        (own_sel_hbm, own_sel_ref), (sum_sel_hbm, sum_sel_ref), (back_hbm, back_ref),
        (scale_hbm, scale_ref), (self_t_hbm, self_t_ref), (neigh_t_hbm, neigh_t_ref),
        (outer_sel_hbm, outer_sel_ref), (outer_scale_hbm, outer_scale_ref),
        (cot_t_hbm, cot_t_ref),
    )
    split = [
        (source.at[b], target.at[b]) for b in range(batches) for source, target in pairs[:3]
    ]
    loads = [
        pltpu.make_async_copy(source, target, sems.at[i])
        for i, (source, target) in enumerate(split + list(pairs[3:]))
    ]
    count = len(split)
    first = loads[0:2] + loads[count : count + 3]
    rest = loads[2:count] + loads[count + 3 :]
    for copy in first + rest:
        copy.start()
    second[:, classes:, :] = jnp.zeros((2, second.shape[1] - classes, hidden), F32)
    for b in range(batches):
        table_t[b] = fetched_ref[:, b].reshape(slots, width).T

    def inputs(b):
        if b == 0:
            first[0].wait()
        own_t = nn(table_t[b], own_sel_ref[b]).astype(BF)
        if b == 0:
            first[1].wait()
            first[2].wait()
        mean_t = (nn(table_t[b], sum_sel_ref[b]) * scale_ref[b]).astype(BF)
        inputs_t[0, :, b * nodes : (b + 1) * nodes] = own_t
        inputs_t[1, :, b * nodes : (b + 1) * nodes] = mean_t
        if b == 0:
            first[3].wait()
            first[4].wait()
        return nn(self_t_ref[...], own_t) + nn(neigh_t_ref[...], mean_t)

    pre = inputs(0)
    for copy in rest:
        copy.wait()
    for b in range(batches):
        if b > 0:
            pre = inputs(b)
        gate = 1.0 / (1.0 + jnp.exp(-pre))
        hidden_t = (pre * gate).astype(BF)
        slope = back_ref[b] * (gate * (1.0 + pre * (1.0 - gate)))
        back_t[:, b * nodes : (b + 1) * nodes] = slope.astype(BF)
        outer_t = (nn(hidden_t, outer_sel_ref[b]) * outer_scale_ref[b]).astype(BF)
        seed_t = hidden_t[:, 0:seeds]
        seeds_t[0, b] = seed_t
        seeds_t[1, b] = outer_t
        self_grad = nt(cot_t_ref[b], seed_t)
        neigh_grad = nt(cot_t_ref[b], outer_t)
        if b == 0:
            second[0, 0:classes, :] = self_grad
            second[1, 0:classes, :] = neigh_grad
        else:
            second[0, 0:classes, :] += self_grad
            second[1, 0:classes, :] += neigh_grad
    sent = 1 - lax.axis_index("core")
    send_ref[0:width, :] = nt(inputs_t[sent], back_t[...]).astype(BF)
    send_ref[width:, :] = second[sent].astype(BF)


def both_passes(fetched, planned, half_rows):
    batches = fetched.shape[1]
    width = fetched.shape[3]
    hidden = planned[6].shape[0]
    seeds = planned[3].shape[2]
    nodes = planned[0].shape[2]
    tail = half_rows - width
    return pl.pallas_call(
        pass_kernel,
        out_shape=(
            struct((2, batches, hidden, seeds), BF),
            struct((half_rows, hidden), BF),
            struct((2, width, batches * nodes), BF),
            struct((hidden, batches * nodes), BF),
            struct((2, tail, hidden), F32),
        ),
        in_specs=[VMEM] + [ANY] * len(planned),
        out_specs=[VMEM] * 5,
        scratch_shapes=[pltpu.VMEM(value.shape, value.dtype) for value in planned]
        + [
            pltpu.VMEM((batches, width, nodes), BF),
            pltpu.SemaphoreType.DMA((len(planned) + 3 * (batches - 1),)),
        ],
        compiler_params=params(40),
        cost_estimate=cost(4_500_000_000, 20_000_000),
        name="both_passes",
    )(fetched, *[in_hbm(value) for value in planned])


def keep_kernel(inputs_t, back_t, second, seeds_t, self_two_ref, neigh_two_ref, keep_ref, logits_ref):
    core = lax.axis_index("core")
    width = inputs_t.shape[1]
    keep_ref[0:width, :] = nt(inputs_t[core], back_t[...])
    keep_ref[width:, :] = second[core]
    for b in range(logits_ref.shape[0]):
        own = nn(self_two_ref[...], seeds_t[0, b])
        logits_ref[b, :, :] = (own + nn(neigh_two_ref[...], seeds_t[1, b])).T


def keep_half(inputs_t, back_t, second, seeds_t, self_two, neigh_two, logit_shape):
    width, nodes = inputs_t.shape[1:]
    tail, hidden = second.shape[1:]
    return pl.pallas_call(
        keep_kernel,
        out_shape=(struct((width + tail, hidden), F32), struct(logit_shape, F32)),
        in_specs=[VMEM] * 6,
        out_specs=[VMEM] * 2,
        compiler_params=params(16),
        cost_estimate=cost(2 * width * hidden * nodes, 5_000_000),
        name="keep_half",
    )(inputs_t, back_t, second, seeds_t, self_two, neigh_two)


def add_kernel(keep_ref, got_ref, out_ref):
    total = (keep_ref[...] + got_ref[...].astype(F32)).astype(BF)
    for j in range(out_ref.shape[0]):
        out_ref[j] = total[:, j * LANES : (j + 1) * LANES]


def add_pair(keep, got):
    return pl.pallas_call(
        add_kernel,
        out_shape=struct((keep.shape[1] // LANES, keep.shape[0], LANES), BF),
        in_specs=[VMEM] * 2,
        out_specs=VMEM,
        compiler_params=params(6),
        cost_estimate=cost(keep.size, keep.size * 8),
        name="add_pair",
    )(keep, got)


def sum_kernel(parts_ref, out_ref):
    total = parts_ref[0].astype(F32)
    for i in range(1, parts_ref.shape[0]):
        total += parts_ref[i].astype(F32)
    out_ref[...] = total.astype(BF)


def sum_parts(parts):
    return pl.pallas_call(
        sum_kernel,
        out_shape=struct(parts.shape[1:], BF),
        in_specs=[VMEM],
        out_specs=VMEM,
        compiler_params=params(3),
        cost_estimate=cost(parts.size, parts.size * 4),
        name="sum_parts",
    )(parts)


def total_kernel(own_ref, next_ref, across_ref, last_ref, out_ref):
    near = own_ref[...].astype(F32) + across_ref[...].astype(F32)
    far = next_ref[...].astype(F32) + last_ref[...].astype(F32)
    total = (near + far).astype(BF)
    for i in range(out_ref.shape[0]):
        out_ref[i] = total


def total_copies(own, got, copies):
    return pl.pallas_call(
        total_kernel,
        out_shape=struct((copies,) + own.shape, BF),
        in_specs=[VMEM] * 4,
        out_specs=VMEM,
        compiler_params=params(3),
        cost_estimate=cost(own.size * copies, own.size * copies * 2),
        name="total_copies",
    )(own, *got)


def unpack_kernel(mine, half_ref, *refs):
    self_one, neigh_one, self_two, neigh_two, head, tail, sems = refs[-7:]
    width = head.shape[0]
    classes = tail.shape[0]
    parts = sems.shape[0] - 1
    block = width // parts
    columns = half_ref.shape[0]

    def place(one, two):
        copies = []
        for i in range(parts):
            here = slice(i * block, (i + 1) * block)
            for j in range(columns):
                head[here, j * LANES : (j + 1) * LANES] = half_ref[j, here, :].astype(F32)
            copies.append(pltpu.make_async_copy(head.at[here], one.at[here], sems.at[i]))
            copies[-1].start()
        for j in range(columns):
            piece = half_ref[j, width : width + classes, :].astype(F32)
            tail[:, j * LANES : (j + 1) * LANES] = piece
        copies.append(pltpu.make_async_copy(tail, two, sems.at[parts]))
        copies[-1].start()
        for copy in copies:
            copy.wait()

    core = lax.axis_index("core")
    slot = core if mine else 1 - core

    @pl.when(slot == 0)
    def _():
        place(self_one, self_two)

    @pl.when(slot != 0)
    def _():
        place(neigh_one, neigh_two)


def unpack(mine, half, one_shape, two_shape, placed=()):
    return pl.pallas_call(
        functools.partial(unpack_kernel, mine),
        out_shape=tuple(pltpu.HBM(shape, F32) for shape in (one_shape,) * 2 + (two_shape,) * 2),
        in_specs=[VMEM] + [ANY] * len(placed),
        out_specs=[ANY] * 4,
        scratch_shapes=[
            pltpu.VMEM(one_shape, F32),
            pltpu.VMEM(two_shape, F32),
            pltpu.SemaphoreType.DMA((5,)),
        ],
        input_output_aliases={1 + i: i for i in range(len(placed))},
        compiler_params=params(5),
        cost_estimate=cost(half.size, half.size * 6),
        name="unpack",
    )(half, *[in_hbm(value) for value in placed])


def exchange(value, axes):
    return lax.all_to_all(value, axes, split_axis=0, concat_axis=0, tiled=True)


def swap_cores(value):
    return lax.ppermute(value, "core", [(0, 1), (1, 0)])


def body(
    features, self_one, neigh_one, self_two, neigh_two, bucket_counts, request_rows,
    layer_targets, inner_slots, outer_slots, outer_degree, cotangent,
):
    batches, _, owners, capacity = request_rows.shape
    width, hidden = self_one.shape
    wanted = request_rows[:, 0].transpose(1, 0, 2).reshape(owners, batches * capacity)
    asked = exchange(wanted, STORE)
    planned = plan(
        bucket_counts[:, 0],
        layer_targets,
        inner_slots.transpose(0, 2, 1),
        outer_slots.transpose(0, 2, 1),
        outer_degree,
        cotangent,
        self_one,
        neigh_one,
        self_two.T,
        neigh_two.T,
    )
    rows = serve(asked, features)
    fetched = exchange(rows.reshape(owners, batches, capacity, width), STORE)
    plane = PLANE
    parties = lax.axis_size(plane)
    far = lax.axis_size("far")
    unit = parties * SUBLANES * LANES // hidden
    half_rows = -(-(width + cotangent.shape[2]) // unit) * unit
    seeds_t, send, inputs_t, back_t, second = both_passes(fetched, planned, half_rows)
    got = swap_cores(send)
    keep, logits = keep_half(
        inputs_t, back_t, second, seeds_t, self_two.T, neigh_two.T, cotangent.shape
    )
    half = add_pair(keep, got)
    own = sum_parts(exchange(half.reshape(parties, -1, LANES), plane))
    got = [
        lax.ppermute(own, "far", [(i, (i + shift) % far) for i in range(far)])
        for shift in range(1, far)
    ]
    mine = exchange(total_copies(own, got, parties), plane).reshape(half.shape)
    other = swap_cores(mine)
    shapes = (self_one.shape, self_two.T.shape)
    grads = unpack(False, other, *shapes, unpack(True, mine, *shapes))
    return (logits, grads[0], grads[1], grads[2].T, grads[3].T)


def solution(mesh):
    stores, trainers = mesh.shape["store"], mesh.shape["trainer"]
    chips = stores // 2
    side = int(chips**0.5)
    split = Mesh(
        mesh.devices.reshape(chips // side, side, 2, trainers // 2, 2), STORE + ("far", "near")
    )
    every = STORE + ("far", "near")
    in_specs = (
        P(STORE, None),
        P(),
        P(),
        P(),
        P(),
        P(None, every, None),
        P(None, every, None, None),
        P(None, every),
        P(None, every, None),
        P(None, every, None),
        P(None, every),
        P(None, every, None),
    )
    out_specs = (P(None, every, None), P(), P(), P(), P())
    return jax.shard_map(
        body, mesh=split, in_specs=in_specs, out_specs=out_specs, check_vma=False
    )
```
